32 devices in a mesh: member: 2 (over y), lon: 4 (over x, core), lat: 4 (over z).
Axes of the slice: x: 2, y: 2, z: 4, core: 2. Of those that a mesh axis runs over, the one named last changes fastest.
Arguments:
- tracer: float32 [150, 128, 1024], P('member', 'lat', 'lon'), parts along dimension 0, may hold values from -6 to 6
- u_flow: float32 [150, 128, 1024], P('member', 'lat', 'lon'), parts along dimension 0, may hold values from -0.25 to 0.25
- v_flow: float32 [150, 128, 1024], P('member', 'lat', 'lon'), parts along dimension 0, may hold values from -0.25 to 0.25
- depth_levels: int32 [256, 1024], P(('member', 'lat'), 'lon'), parts along dimension 0, may hold values from 0 to 75
- class_index: int32 [150, 128, 1024], P('member', 'lat', 'lon'), parts along dimension 0, may hold values from 0 to 191
- basin_index: int32 [256, 1024], P(('member', 'lat'), 'lon'), parts along dimension 0, may hold values from 0 to 4
- level_thickness: float32 [75], replicated, may hold values from 0.5 to 2
Outputs:
- tracer_next: float32 [150, 128, 1024], P('member', 'lat', 'lon'), parts along dimension 0
- overturning: float32 [10, 128, 192], P('member', ('lat', 'lon')), parts along dimension 0
- tendency_sum: float32 [10, 128, 192], P('member', ('lat', 'lon')), parts along dimension 0
The draws below stay inside these ranges and needn't reach their ends.
There are 2 independent parts, one for each index of `member`. The reference program is written for one: setup_inputs(seed, part) draws one part's arguments, and reference() takes and returns one part's arrays. A program takes and returns all parts, laid end to end along the dimension named above; an argument that names none is the same for every part. Nothing has to cross between parts.
All inputs are finite; a program needn't handle non-finite values.
Results may differ from the reference program's by a relative error of at most 0.0003.
Values sent between devices are 32-bit elements; how exact they have to be, the bound alone decides.
No kernel may reach another device: no remote copies, remote signals or barrier semaphores. Data moves between devices by JAX's collectives and lax.ppermute only.
A program may use at most 128 MiB of HBM per device.

```python
import math
import jax
import jax.numpy as jnp
from jax import lax

K = 75
C = 192
B = 5
NI = 1024
NJ = 128


def place_ends(values, key, least, largest):
    shape = values.shape
    spot = [jax.random.randint(jax.random.fold_in(key, axis), (), 0, shape[axis]) for axis in range(len(shape))]
    values = values.at[tuple(spot)].set(least)
    longest = shape.index(max(shape))
    spot[longest] = (spot[longest] + 1) % shape[longest]
    return values.at[tuple(spot)].set(largest)


def shard_levels(stream_key, shape, shards, low, high):
    def one(dim, parts):
        heights = jax.random.uniform(jax.random.fold_in(jax.random.fold_in(stream_key, 6), dim), (parts,), jnp.float32, low / len(shards), high / len(shards))
        return jnp.repeat(jnp.exp(heights), shape[dim] // parts).reshape((-1,) + (1,) * (len(shape) - dim - 1))

    loudness = one(*shards[0])
    for cut in shards[1:]:
        loudness = loudness * one(*cut)
    return loudness


def bell_draw(key, shape, spread, bound, pieces=(), kind=jnp.bfloat16):
    result = spread * jax.random.normal(key, shape, jnp.float32)
    if pieces:
        result = result * shard_levels(key, shape, pieces, -0.22, 0.18)
    return jnp.clip(result, -bound, bound).astype(kind)


def setup_inputs(seed: int = 0, part: int = 0) -> dict:
    streams_of = jax.random.split(jax.random.key(seed), 8)
    part_splits = jax.random.split(jax.random.fold_in(streams_of[7], part), 8)
    return {
        "tracer": bell_draw(part_splits[0], (K, NJ, NI), 1.0, 6.0, ((1, 4), (2, 4)), jnp.float32),
        "u_flow": jnp.clip(jax.random.uniform(part_splits[1], (K, NJ, NI), jnp.float32, -0.25, 0.25) * shard_levels(part_splits[1], (K, NJ, NI), ((1, 4), (2, 4)), -0.4, 0.0), -0.25, 0.25),
        "v_flow": jnp.clip(jax.random.uniform(part_splits[2], (K, NJ, NI), jnp.float32, -0.25, 0.25) * shard_levels(part_splits[2], (K, NJ, NI), ((1, 4), (2, 4)), -0.4, 0.0), -0.25, 0.25),
        "depth_levels": place_ends(jax.random.randint(part_splits[3], (NJ, NI), 0, K + 1), jax.random.fold_in(part_splits[3], 1), 0, K).astype(jnp.int32),
        "class_index": place_ends(jax.random.randint(part_splits[4], (K, NJ, NI), 0, C), jax.random.fold_in(part_splits[4], 1), 0, C - 1).astype(jnp.int32),
        "basin_index": place_ends(jax.random.randint(part_splits[5], (NJ, NI), 0, B), jax.random.fold_in(part_splits[5], 1), 0, B - 1).astype(jnp.int32),
        "level_thickness": jnp.clip(jnp.exp(jax.random.uniform(streams_of[6], (K,), jnp.float32, math.log(0.5), math.log(2.0))), 0.5, 2.0),
    }


DIFFUSION = 0.1

def face_fluxes(tracer_pad, speed_pad, wet_pad, length, along):

    def window(array, offset):
        return lax.slice_in_dim(array, offset, offset + length + 1, axis=along)
    behind = window(tracer_pad, 0)
    here = window(tracer_pad, 1)
    ahead = window(tracer_pad, 2)
    beyond = window(tracer_pad, 3)
    speed = window(speed_pad, 1)
    open_face = window(wet_pad, 1) * window(wet_pad, 2)
    advect = speed * (7.0 * (here + ahead) - (behind + beyond)) / 12.0
    upwind = jnp.abs(speed) * (beyond - 3.0 * ahead + 3.0 * here - behind) / 12.0
    return open_face * (advect + upwind - DIFFUSION * (ahead - here))

def divergence(fluxes, along):
    extent = fluxes.shape[along] - 1
    return lax.slice_in_dim(fluxes, 1, extent + 1, axis=along) - lax.slice_in_dim(fluxes, 0, extent, axis=along)

def reference(tracer, u_flow, v_flow, depth_levels, class_index, basin_index, level_thickness):
    depth_pad = jnp.pad(depth_levels, 2)
    row_ids = lax.broadcasted_iota(jnp.int32, (NJ, NI), 0)
    segment_base = (row_ids * B + basin_index) * C

    def level_step(totals, inputs):
        level, tracer_level, east_level, north_level, class_level, thick_level = inputs
        wet = (level < depth_levels).astype(jnp.float32)
        wet_pad = (level < depth_pad).astype(jnp.float32)
        masked = wet * tracer_level
        tracer_pad = jnp.pad(masked, 2)
        east_pad = jnp.pad(east_level, 2)
        north_pad = jnp.pad(north_level, 2)
        zonal = face_fluxes(tracer_pad[2:-2], east_pad[2:-2], wet_pad[2:-2], NI, 1)
        merid = face_fluxes(tracer_pad[:, 2:-2], north_pad[:, 2:-2], wet_pad[:, 2:-2], NJ, 0)
        updated = wet * (masked - divergence(zonal, 1) - divergence(merid, 0))
        transport = north_level * wet * wet_pad[3:-1, 2:-2] * thick_level
        change = (updated - masked) * thick_level
        segment = (segment_base + class_level).ravel()
        binned = jnp.stack([jax.ops.segment_sum(transport.ravel(), segment, num_segments=NJ * B * C), jax.ops.segment_sum(change.ravel(), segment, num_segments=NJ * B * C)])
        return (totals + binned, updated)
    start = jnp.zeros((2, NJ * B * C), jnp.float32)
    levels = jnp.arange(K, dtype=jnp.int32)
    totals, tracer_next = lax.scan(level_step, start, (levels, tracer, u_flow, v_flow, class_index, level_thickness))
    binned = totals.reshape(2, NJ, B, C).transpose(0, 2, 1, 3)
    unit = 1.0 / math.sqrt(NI * K)
    overturning = jnp.flip(jnp.cumsum(jnp.flip(binned[0], 2), axis=2), 2) * (16.0 * unit)
    tendency_sum = jnp.cumsum(binned[1], axis=1) * (4.0 * unit)
    return (tracer_next, overturning, tendency_sum)
```

```python
import functools
import math

import jax
import jax.numpy as jnp
from jax import lax
from jax.experimental import pallas as pl
from jax.experimental.pallas import tpu as pltpu
from jax.sharding import PartitionSpec as P

C = 192
B = 5
DIFFUSION = 0.1

LANES = 128
SLOTS = 4
PER_TILE = LANES // SLOTS
LOW = 64
HIGH = C // LOW
HEADS = 16
VMEM = 56 << 20
F32 = jnp.float32
BF16 = jnp.bfloat16


def lane_ids(shape):
    return lax.broadcasted_iota(jnp.int32, shape, len(shape) - 1)


def row_ids(shape):
    return lax.broadcasted_iota(jnp.int32, shape, len(shape) - 2)


def pack_kernel(tracer_ref, east_ref, north_ref, depth_ref, lon_ref, up_ref, down_ref):
    levels, rows, cols = tracer_ref.shape
    tiles = pl.cdiv(levels, PER_TILE)
    lon_ref[...] = jnp.zeros_like(lon_ref)
    lanes = lane_ids((rows, LANES))

    def level(k, carry):
        masked = jnp.where(k < depth_ref[...], tracer_ref[k], 0.0)
        ends = jnp.where(lanes < LANES // 2, masked[:, :LANES], masked[:, cols - LANES :])
        slot = k % PER_TILE
        turned = pltpu.roll(ends, (SLOTS * slot + 2) % LANES, 1)
        tile = pl.ds(pl.multiple_of(k // PER_TILE * LANES, LANES), LANES)
        lon_ref[:, tile] = jnp.where(lanes // SLOTS == slot, turned, lon_ref[:, tile])
        speed = pltpu.roll(east_ref[k], (k + 1) % LANES, 1)
        last = pl.ds(tiles * LANES, LANES)
        lon_ref[:, last] = jnp.where(lanes == k, speed, lon_ref[:, last])
        here = pl.ds(k, 1)
        up_ref[0, here, :] = masked[rows - 2 : rows - 1]
        up_ref[1, here, :] = masked[rows - 1 : rows]
        up_ref[2, here, :] = north_ref[k, 7:8, :]
        down_ref[0, here, :] = masked[0:1]
        down_ref[1, here, :] = masked[1:2]
        return carry

    lax.fori_loop(0, levels, level, 0)
    depth = depth_ref[...].astype(F32)
    last = pl.ds(tiles * LANES, LANES)
    from_end = pltpu.roll(depth[:, cols - LANES :], LANES - 1, 1)
    from_start = pltpu.roll(depth[:, :LANES], LANES - 1, 1)
    lon_ref[:, last] = jnp.where(
        lanes == LANES - 2, from_end, jnp.where(lanes == LANES - 1, from_start, lon_ref[:, last])
    )
    up_ref[0, levels : levels + 1, :] = depth[rows - 1 : rows]
    down_ref[0, levels : levels + 1, :] = depth[0:1]


def pack(tracer, u_flow, v_flow, depth):
    levels, rows, cols = tracer.shape
    tiles = pl.cdiv(levels, PER_TILE)
    tall = (levels + 8) // 8 * 8
    return pl.pallas_call(
        pack_kernel,
        grid=(1,),
        in_specs=[
            pl.BlockSpec((levels, rows, cols), lambda i: (0, 0, 0)),
            pl.BlockSpec((levels, rows, LANES), lambda i: (0, 0, cols // LANES - 1)),
            pl.BlockSpec((levels, 8, cols), lambda i: (0, rows // 8 - 1, 0)),
            pl.BlockSpec((rows, cols), lambda i: (0, 0)),
        ],
        out_specs=[
            pl.BlockSpec((rows, (tiles + 1) * LANES), lambda i: (0, 0)),
            pl.BlockSpec((3, tall, cols), lambda i: (0, 0, 0)),
            pl.BlockSpec((2, tall, cols), lambda i: (0, 0, 0)),
        ],
        out_shape=[
            jax.ShapeDtypeStruct((rows, (tiles + 1) * LANES), F32),
            jax.ShapeDtypeStruct((3, tall, cols), F32),
            jax.ShapeDtypeStruct((2, tall, cols), F32),
        ],
        compiler_params=pltpu.CompilerParams(vmem_limit_bytes=VMEM),
        name="pack_edges",
    )(tracer, u_flow, v_flow, depth)


def face_flux(value, speed, closed, axis):
    extent = value.shape[axis]
    step = pltpu.roll(value, extent - 1, axis)
    pair = value + step
    slope = step - value
    back = pltpu.roll(slope, 1, axis)
    front = pltpu.roll(slope, extent - 1, axis)
    twelfth = speed * (1.0 / 12.0)
    advect = twelfth * (6.0 * pair + (back - front))
    upwind = jnp.abs(twelfth) * (front - 2.0 * slope + back)
    flux = advect + upwind - DIFFUSION * slope
    return jnp.where(closed, 0.0, flux)


def main_kernel(
    thick_ref, tracer_ref, east_ref, north_ref, class_ref, depth_ref, basin_ref,
    west_ref, far_ref, south_ref, ahead_ref,
    next_ref, bins_ref,
    edge_ref, zonal_ref, merid_ref, head_ref, flow_hi, flow_lo, gain_hi, gain_lo, head_key, low_key, sums_ref,
):
    chunk = pl.program_id(0)
    per, rows, cols = tracer_ref.shape
    levels = thick_ref.shape[0]
    tiles = pl.cdiv(levels, PER_TILE)
    last = tiles * LANES

    @pl.when(chunk == 0)
    def _():
        lanes = lane_ids((rows, last))
        edge_ref[...] = jnp.where(lanes % SLOTS < 2, west_ref[:, :last], far_ref[:, :last])
        depth = depth_ref[...].astype(F32)
        west = west_ref[:, last + LANES - 2 : last + LANES - 1]
        far = far_ref[:, last + LANES - 1 : last + LANES]
        side = lane_ids((rows, LANES))
        halo = jnp.where(side == 0, far, west)
        wide = jnp.concatenate([depth, halo], 1)
        zonal_ref[...] = jnp.minimum(wide, pltpu.roll(wide, cols + LANES - 1, 1)).astype(jnp.int32)
        ends = row_ids((8, cols))
        halo = jnp.where(ends == 0, ahead_ref[0, levels : levels + 1, :], south_ref[0, levels : levels + 1, :])
        tall = jnp.concatenate([depth, halo], 0)
        merid_ref[...] = jnp.minimum(tall, pltpu.roll(tall, rows + 7, 0)).astype(jnp.int32)
        head_ref[...] = basin_ref[...] * HIGH

    def level(q, carry):
        k = chunk * per + q
        depth = depth_ref[...]
        wet = k < depth
        masked = jnp.where(wet, tracer_ref[q], 0.0)
        thick = thick_ref[k]
        tile = pl.ds(pl.multiple_of(k // PER_TILE * LANES, LANES), LANES)
        slot = k % PER_TILE
        halo = pltpu.roll(edge_ref[:, tile], (2 * LANES - 2 - SLOTS * slot) % LANES, 1)
        speed_halo = pltpu.roll(west_ref[:, last:], LANES - 1 - k, 1)
        zonal = face_flux(
            jnp.concatenate([masked, halo], 1),
            jnp.concatenate([east_ref[q], speed_halo], 1),
            k >= zonal_ref[...],
            1,
        )
        zonal_div = (zonal - pltpu.roll(zonal, 1, 1))[:, :cols]
        here = pl.ds(k, 1)
        side = row_ids((8, cols))
        halo = jnp.where(
            side == 0,
            ahead_ref[0, here, :],
            jnp.where(
                side == 1, ahead_ref[1, here, :], jnp.where(side == 6, south_ref[0, here, :], south_ref[1, here, :])
            ),
        )
        speed_halo = jnp.broadcast_to(south_ref[2, here, :], (8, cols))
        north = north_ref[q]
        faces = merid_ref[...]
        merid = face_flux(
            jnp.concatenate([masked, halo], 0), jnp.concatenate([north, speed_halo], 0), k >= faces, 0
        )
        merid_div = (merid - pltpu.roll(merid, 1, 0))[:rows]
        updated = jnp.where(wet, masked - zonal_div - merid_div, 0.0)
        next_ref[q] = updated
        flow = jnp.where(k < faces[:rows], north * thick, 0.0)
        gain = (updated - masked) * thick
        upper = flow.astype(BF16).astype(F32)
        flow_hi[q] = upper
        flow_lo[q] = flow - upper
        upper = gain.astype(BF16).astype(F32)
        gain_hi[q] = upper
        gain_lo[q] = gain - upper
        classes = class_ref[q]
        head_key[q] = (head_ref[...] + classes // LOW).astype(F32)
        low_key[q] = (classes % LOW).astype(F32)
        return carry

    lax.fori_loop(0, per, level, 0)

    heads = row_ids((HEADS, cols)).astype(F32).astype(BF16)
    lows = row_ids((LOW, cols)).astype(F32).astype(BF16)
    ones = jnp.ones((LOW, cols), BF16)
    none = jnp.zeros((LOW, cols), BF16)
    unroll = 8

    def spread(ref, q, r, count):
        return jnp.broadcast_to(ref[q, pl.ds(r, 1), :], (count, cols)).astype(BF16)

    def bin_row(r):
        left, right = ([], [])
        for q in range(per):
            hot = spread(head_key, q, r, HEADS) == heads
            left.append(
                jnp.concatenate(
                    [
                        jnp.where(hot, spread(ref, q, r, HEADS), none[:HEADS])
                        for ref in (flow_hi, flow_lo, gain_hi, gain_lo)
                    ],
                    0,
                )
            )
            right.append(jnp.where(spread(low_key, q, r, LOW) == lows, ones, none))
        return lax.dot_general(
            jnp.concatenate(left, 1),
            jnp.concatenate(right, 1),
            (((1,), (1,)), ((), ())),
            preferred_element_type=F32,
        )

    def some_rows(start, carry):
        for p in range(unroll):
            r = start * unroll + p
            total = bin_row(r)
            sums_ref[r] = jnp.where(chunk == 0, total, total + sums_ref[r])
        return carry

    lax.fori_loop(0, rows // unroll, some_rows, 0)

    @pl.when(chunk == pl.num_programs(0) - 1)
    def _():
        def finish(r, running):
            total = sums_ref[r]
            flow = total[:HEADS] + total[HEADS : 2 * HEADS]
            running = running + total[2 * HEADS : 3 * HEADS] + total[3 * HEADS :]
            bins_ref[r] = jnp.concatenate([flow, running], 1)
            return running

        lax.fori_loop(0, rows, finish, jnp.zeros((HEADS, LOW), F32), unroll=4)


def step_and_bin(thick, tracer, u_flow, v_flow, classes, depth, basins, west, far, south, ahead):
    levels, rows, cols = tracer.shape
    per = next(n for n in range(15, 0, -1) if levels % n == 0)
    block = pl.BlockSpec((per, rows, cols), lambda i: (i, 0, 0))

    def whole(array):
        return pl.BlockSpec(array.shape, lambda i: (0,) * array.ndim)

    stage = pltpu.VMEM((per, rows, cols), F32)
    tiles = pl.cdiv(levels, PER_TILE)
    return pl.pallas_call(
        main_kernel,
        grid=(levels // per,),
        in_specs=[pl.BlockSpec(memory_space=pltpu.SMEM)]
        + [block] * 4
        + [whole(x) for x in (depth, basins, west, far, south, ahead)],
        out_specs=[block, pl.BlockSpec((rows, HEADS, 2 * LOW), lambda i: (0, 0, 0))],
        out_shape=[
            jax.ShapeDtypeStruct((levels, rows, cols), F32),
            jax.ShapeDtypeStruct((rows, HEADS, 2 * LOW), F32),
        ],
        scratch_shapes=[
            pltpu.VMEM((rows, tiles * LANES), F32),
            pltpu.VMEM((rows, cols + LANES), jnp.int32),
            pltpu.VMEM((rows + 8, cols), jnp.int32),
            pltpu.VMEM((rows, cols), jnp.int32),
            stage, stage, stage, stage, stage, stage,
            pltpu.VMEM((rows, 4 * HEADS, LOW), F32),
        ],
        compiler_params=pltpu.CompilerParams(vmem_limit_bytes=VMEM),
        name="step_and_bin",
    )(thick, tracer, u_flow, v_flow, classes, depth, basins, west, far, south, ahead)


def close_kernel(scales, pieces, carries, *refs):
    piece_refs, carry_refs = (refs[:pieces], refs[pieces : pieces + carries])
    over_ref, tend_ref, up_ref, run_ref = refs[pieces + carries :]
    share = piece_refs[0].shape[0]
    total = piece_refs[0][...]
    for ref in piece_refs[1:]:
        total = total + ref[...]
    total = total.reshape(share * HEADS, 2 * LOW)
    source = row_ids((2 * LOW, 2 * LOW))
    target = lane_ids((2 * LOW, 2 * LOW))
    after = (source < LOW) & ((target >= LOW) | (source >= target))
    up_ref[...] = jnp.dot(
        total, after.astype(F32), precision=lax.Precision.HIGHEST, preferred_element_type=F32
    )
    run_ref[...] = total
    carry = jnp.zeros((HEADS, 2 * LOW), F32)
    for ref in carry_refs:
        carry = carry + ref[...]
    for b in range(B):
        above = jnp.zeros((share, LOW), F32)
        for high in reversed(range(HIGH)):
            head = b * HIGH + high
            rows = up_ref[pl.ds(head, share, HEADS), :]
            over_ref[b, :, high * LOW : (high + 1) * LOW] = (rows[:, :LOW] + above) * scales[0]
            above = above + rows[:, LOW:]
            rows = run_ref[pl.ds(head, share, HEADS), :] + carry[head : head + 1]
            tend_ref[b, :, high * LOW : (high + 1) * LOW] = rows[:, LOW:] * scales[1]


def close(pieces, carries, scales):
    share = pieces[0].shape[0]
    out = jax.ShapeDtypeStruct((B, share, C), F32)
    scratch = pltpu.VMEM((share * HEADS, 2 * LOW), F32)
    return pl.pallas_call(
        functools.partial(close_kernel, scales, len(pieces), len(carries)),
        out_shape=[out, out],
        scratch_shapes=[scratch, scratch],
        name="close_sums",
    )(*pieces, *carries)


def body(tracer, u_flow, v_flow, depth_levels, class_index, basin_index, level_thickness):
    levels, rows, cols = tracer.shape
    lons, lats = (lax.axis_size("lon"), lax.axis_size("lat"))
    here = lax.axis_index("lon")

    def ahead(count):
        return [(i, i + 1) for i in range(count - 1)]

    def behind(count):
        return [(i + 1, i) for i in range(count - 1)]

    lon_edge, up_edge, down_edge = pack(tracer, u_flow, v_flow, depth_levels)
    west = lax.ppermute(lon_edge, "lon", ahead(lons))
    far = lax.ppermute(lon_edge, "lon", behind(lons))
    south = lax.ppermute(up_edge, "lat", ahead(lats))
    north = lax.ppermute(down_edge, "lat", behind(lats))
    tracer_next, bins = step_and_bin(
        level_thickness, tracer, u_flow, v_flow, class_index, depth_levels, basin_index, west, far, south, north
    )
    share = rows // lons
    block_total = jnp.where(lane_ids((HEADS, 2 * LOW)) < LOW, 0.0, bins[rows - 1])
    carry = jnp.zeros_like(block_total)
    for d in range(1, lats):
        carry = carry + lax.ppermute(block_total, "lat", [(i, i + d) for i in range(lats - d)])
    bins = bins + carry
    blocks = bins.reshape(lons, share, HEADS, 2 * LOW)

    def piece(owner):
        return lax.dynamic_index_in_dim(blocks, owner, 0, False)

    pieces = [piece(here)]
    for d in range(1, lons):
        pieces.append(lax.ppermute(piece((here + d) % lons), "lon", [(i, (i + d) % lons) for i in range(lons)]))
    unit = 1.0 / math.sqrt(cols * lons * levels)
    overturning, tendency = close(pieces, [], (16.0 * unit, 4.0 * unit))
    return (tracer_next, overturning, tendency)


def solution(mesh):
    return jax.shard_map(
        body,
        mesh=mesh,
        in_specs=(
            P("member", "lat", "lon"),
            P("member", "lat", "lon"),
            P("member", "lat", "lon"),
            P(("member", "lat"), "lon"),
            P("member", "lat", "lon"),
            P(("member", "lat"), "lon"),
            P(),
        ),
        out_specs=(
            P("member", "lat", "lon"),
            P("member", ("lat", "lon"), None),
            P("member", ("lat", "lon"), None),
        ),
        check_vma=False,
    )
```

```python
import functools
import math

import jax
import jax.numpy as jnp
from jax import lax
from jax.experimental import pallas as pl
from jax.experimental.pallas import tpu as pltpu
from jax.sharding import PartitionSpec as P

C = 192
B = 5
DIFFUSION = 0.1

LANES = 128
LOW = 64
HIGH = C // LOW
HEADS = 16
PER = 5
VMEM = 56 << 20
F32 = jnp.float32
BF16 = jnp.bfloat16


def lane_ids(shape):
    return lax.broadcasted_iota(jnp.int32, shape, len(shape) - 1)


def row_ids(shape):
    return lax.broadcasted_iota(jnp.int32, shape, len(shape) - 2)


def flux_of(here, slope, bend, bend_ahead, speed):
    value = here + 0.5 * slope - jnp.where(speed > 0.0, bend, bend_ahead)
    return speed * value - DIFFUSION * slope


def sixth(behind, here, ahead):
    return ((ahead - here) - (here - behind)) * (1.0 / 6.0)


def pack_kernel(tracer_ref, east_ref, north_ref, depth_ref, right_ref, left_ref, up_ref, down_ref):
    per, rows, cols = tracer_ref.shape
    first = pl.program_id(0) * per
    levels = pl.num_programs(0) * per
    lanes = lane_ids((rows, LANES))

    @pl.when(first == 0)
    def _():
        right_ref[...] = jnp.zeros_like(right_ref)
        left_ref[...] = jnp.zeros_like(left_ref)

    depth = depth_ref[...]
    kept = [right_ref[:, i * LANES : (i + 1) * LANES] for i in range(3)]
    kept += [left_ref[:, i * LANES : (i + 1) * LANES] for i in range(2)]
    for q in range(per):
        k = first + q
        masked = jnp.where(k < depth, tracer_ref[q], 0.0)
        near, away = (masked[:, :LANES], masked[:, cols - LANES :])
        turned = [
            pltpu.roll(away, k + 2, 1),
            pltpu.roll(away, k + 1, 1),
            pltpu.roll(east_ref[q], k + 1, 1),
            pltpu.roll(near, k, 1),
            pltpu.roll(near, k + LANES - 1, 1),
        ]
        kept = [jnp.where(lanes == k, new, old) for new, old in zip(turned, kept)]
        here = pl.ds(k, 1)
        up_ref[0, here, :] = masked[rows - 2 : rows - 1]
        up_ref[1, here, :] = masked[rows - 1 : rows]
        up_ref[2, here, :] = north_ref[q, 7:8, :]
        down_ref[0, here, :] = masked[0:1]
        down_ref[1, here, :] = masked[1:2]
    final = first + per == levels
    deep = depth.astype(F32)
    kept[2] = jnp.where(final & (lanes == LANES - 1), deep[:, cols - LANES :], kept[2])
    kept[3] = jnp.where(final & (lanes == LANES - 1), pltpu.roll(deep[:, :LANES], LANES - 1, 1), kept[3])
    for i in range(3):
        right_ref[:, i * LANES : (i + 1) * LANES] = kept[i]
    for i in range(2):
        left_ref[:, i * LANES : (i + 1) * LANES] = kept[3 + i]

    @pl.when(final)
    def _():
        up_ref[0, pl.ds(levels, 1), :] = deep[rows - 1 : rows]
        down_ref[0, pl.ds(levels, 1), :] = deep[0:1]


def pack(tracer, u_flow, v_flow, depth):
    levels, rows, cols = tracer.shape
    per = next(n for n in range(15, 0, -1) if levels % n == 0)
    tall = (levels + 8) // 8 * 8
    shapes = [(rows, 3 * LANES), (rows, 2 * LANES), (3, tall, cols), (2, tall, cols)]
    return pl.pallas_call(
        pack_kernel,
        grid=(levels // per,),
        in_specs=[
            pl.BlockSpec((per, rows, cols), lambda i: (i, 0, 0)),
            pl.BlockSpec((per, rows, LANES), lambda i: (i, 0, cols // LANES - 1)),
            pl.BlockSpec((per, 8, cols), lambda i: (i, rows // 8 - 1, 0)),
            pl.BlockSpec((rows, cols), lambda i: (0, 0)),
        ],
        out_specs=[pl.BlockSpec(s, lambda i, n=len(s): (0,) * n) for s in shapes],
        out_shape=[jax.ShapeDtypeStruct(s, F32) for s in shapes],
        compiler_params=pltpu.CompilerParams(vmem_limit_bytes=VMEM),
        name="pack_edges",
    )(tracer, u_flow, v_flow, depth)


def main_kernel(
    place_ref, thick_ref, depth_ref, basin_ref,
    right_ref, left_ref, up_ref, down_ref, west_ref, far_ref, south_ref, ahead_ref,
    tracer_hbm, east_hbm, north_hbm, class_hbm,
    *refs,
):
    next_hbm, *piece_refs = refs[: len(refs) - 19 - 12]
    (
        tracer_ref, east_ref, north_ref, class_ref, next_ref, in_sem, out_sem,
        head_ref, zonal_ref, merid_ref, far_value, far_bend, west_slope, west_flux, ahead_bend, south_flux,
        sums_ref, tall_ref, share_ref,
    ) = refs[len(refs) - 19 - 12 : len(refs) - 12]
    stages = refs[len(refs) - 12 :]
    levels, rows, cols = tracer_ref.shape
    halves = cols // LANES
    per = stages[0].shape[0]
    chunks = levels // per
    parts = len(piece_refs)
    share = rows // parts

    bounds = [(0, per)] + [(per * (2 * i + 1), min(2 * per, levels - per * (2 * i + 1))) for i in range(chunks // 2)]
    size = {n for _, n in bounds[1:]}
    assert len(size) == 1
    size = size.pop()

    def span(piece):
        if isinstance(piece, int) and piece == 0:
            return pl.ds(0, per)
        return pl.ds(per + (piece - 1) * size, size)

    sources = ((tracer_hbm, tracer_ref), (east_hbm, east_ref), (north_hbm, north_ref), (class_hbm, class_ref))

    def copies_in(piece):
        return [
            pltpu.make_async_copy(src.at[span(piece)], dst.at[span(piece)], in_sem.at[piece, i])
            for i, (src, dst) in enumerate(sources)
        ]

    def copy_out(piece):
        return pltpu.make_async_copy(next_ref.at[span(piece)], next_hbm.at[span(piece)], out_sem.at[piece])

    pieces = len(bounds)
    for piece in range(pieces):
        for copy in copies_in(piece):
            copy.start()

    lanes = lane_ids((rows, LANES))
    right = [right_ref[:, i * LANES : (i + 1) * LANES] for i in range(3)]
    left = [left_ref[:, i * LANES : (i + 1) * LANES] for i in range(2)]
    west = [west_ref[:, i * LANES : (i + 1) * LANES] for i in range(3)]
    far = [far_ref[:, i * LANES : (i + 1) * LANES] for i in range(2)]
    west_depth = west[2][:, LANES - 1 :]
    far_depth = far[0][:, LANES - 1 :]
    far_value[...] = far[0]
    far_bend[...] = sixth(right[1], far[0], far[1])
    slope = left[0] - west[1]
    west_slope[...] = slope
    flux = flux_of(west[1], slope, sixth(west[0], west[1], left[0]), sixth(west[1], left[0], left[1]), west[2])
    depth = depth_ref[...].astype(F32)
    faces = jnp.minimum(west_depth, depth[:, :1])
    west_flux[...] = jnp.where(lanes.astype(F32) < faces, flux, 0.0)
    wide = lane_ids((rows, cols))
    beside = jnp.where(wide == cols - 1, far_depth, pltpu.roll(depth, cols - 1, 1))
    zonal_ref[...] = jnp.minimum(depth, beside).astype(jnp.int32)

    ahead_bend[...] = sixth(up_ref[1], ahead_ref[0], ahead_ref[1])
    behind, here, first, second = (south_ref[0], south_ref[1], down_ref[0], down_ref[1])
    flux = flux_of(here, first - here, sixth(behind, here, first), sixth(here, first, second), south_ref[2])
    faces = jnp.minimum(south_ref[0, levels : levels + 1, :], depth[0:1])
    steps = row_ids(flux.shape).astype(F32)
    south_flux[...] = jnp.where(steps < faces, flux, 0.0)
    above = pltpu.roll(depth, rows - 1, 0)
    above = jnp.where(row_ids((rows, cols)) == rows - 1, ahead_ref[0, levels : levels + 1, :], above)
    merid_ref[...] = jnp.minimum(depth, above).astype(jnp.int32)
    head_ref[...] = basin_ref[...] * HIGH

    top = 8
    inner = pl.ds(top, rows)

    def level(chunk, q, stage):
        flow_hi, flow_lo, gain_hi, gain_lo, head_key, low_key = stage
        k = chunk * per + q
        thick = thick_ref[k]
        here = pl.ds(k, 1)
        edge = lane_ids((rows, LANES))
        at_end, at_start = (edge == LANES - 1, edge == 0)

        def split(array):
            return [array[:, h * LANES : (h + 1) * LANES] for h in range(halves)]

        def turn_back(blocks, outside):
            turned = [pltpu.roll(x, LANES - 1, 1) for x in blocks] + [outside]
            return [jnp.where(at_end, turned[h + 1], turned[h]) for h in range(halves)]

        def turn_on(blocks, outside):
            turned = [outside] + [pltpu.roll(x, 1, 1) for x in blocks]
            return [jnp.where(at_start, turned[h], turned[h + 1]) for h in range(halves)]

        def to_end(ref):
            return pltpu.roll(ref[...], LANES - 1 - k, 1)

        def to_start(ref):
            return pltpu.roll(ref[...], LANES - k, 1)

        depth = split(depth_ref[...])
        raw = split(tracer_ref[k])
        wet = [k < d for d in depth]
        masked = [jnp.where(w, x, 0.0) for w, x in zip(wet, raw)]

        ahead = turn_back(masked, to_end(far_value))
        slope = [a - x for a, x in zip(ahead, masked)]
        slope_behind = turn_on(slope, to_start(west_slope))
        bend = [(a - b) * (1.0 / 6.0) for a, b in zip(slope, slope_behind)]
        bend_ahead = turn_back(bend, to_end(far_bend))
        speed = split(east_ref[k])
        shut = [k >= d for d in split(zonal_ref[...])]
        flux = [
            jnp.where(s, 0.0, flux_of(*x)) for s, *x in zip(shut, masked, slope, bend, bend_ahead, speed)
        ]
        flux_behind = turn_on(flux, to_start(west_flux))
        left_over = [m - (a - b) for m, a, b in zip(masked, flux, flux_behind)]

        north = split(north_ref[k])
        shut = [k >= d for d in split(merid_ref[...])]
        classes = split(class_ref[k])
        heads = split(head_ref[...])
        below, over = (split(south_ref[1, here, :]), split(ahead_ref[0, here, :]))
        over_bend, below_flux = (split(ahead_bend[here, :]), split(south_flux[here, :]))
        for h in range(halves):
            part = slice(h * LANES, (h + 1) * LANES)
            rows_of = tall_ref.at[q, h]
            rows_of[0, inner, :] = masked[h]
            rows_of[0, top - 1 : top, :] = below[h]
            rows_of[0, top + rows : top + rows + 1, :] = over[h]
            slope = rows_of[0, pl.ds(top + 1, rows), :] - masked[h]
            slope_behind = masked[h] - rows_of[0, pl.ds(top - 1, rows), :]
            bend = (slope - slope_behind) * (1.0 / 6.0)
            rows_of[1, inner, :] = bend
            rows_of[1, top + rows : top + rows + 1, :] = over_bend[h]
            bend_ahead = rows_of[1, pl.ds(top + 1, rows), :]
            flux = jnp.where(shut[h], 0.0, flux_of(masked[h], slope, bend, bend_ahead, north[h]))
            rows_of[2, inner, :] = flux
            rows_of[2, top - 1 : top, :] = below_flux[h]
            flux_behind = rows_of[2, pl.ds(top - 1, rows), :]
            updated = jnp.where(wet[h], left_over[h] - (flux - flux_behind), 0.0)
            next_ref[k, :, part] = updated
            flow = jnp.where(shut[h], 0.0, north[h] * thick)
            gain = (updated - masked[h]) * thick
            upper = flow.astype(BF16).astype(F32)
            flow_hi[q, :, part] = flow
            flow_lo[q, :, part] = flow - upper
            upper = gain.astype(BF16).astype(F32)
            gain_hi[q, :, part] = gain
            gain_lo[q, :, part] = gain - upper
            head_key[q, :, part] = (heads[h] + (classes[h] >> 6)).astype(F32)
            low_key[q, :, part] = (classes[h] & (LOW - 1)).astype(F32)

    half = HEADS // 2
    order = row_ids((HEADS, cols))
    heads = [(order % half + g * half).astype(F32).astype(BF16) for g in range(2)]
    lows = row_ids((LOW, cols)).astype(F32).astype(BF16)
    ones = jnp.ones((LOW, cols), BF16)
    none = jnp.zeros((LOW, cols), BF16)

    def spread(ref, q, r, count):
        return jnp.broadcast_to(ref[q, r : r + 1, :], (count, cols))

    def bin_row(r, stage, fresh):
        *terms, head_key, low_key = stage
        first, second = ([], [])
        for q in range(per):
            key = spread(head_key, q, r, HEADS).astype(BF16)
            hot = [key == g for g in heads]
            tiles = []
            for upper, lower in (terms[:2], terms[2:]):
                value = jnp.concatenate([spread(upper, q, r, half), spread(lower, q, r, half)], 0).astype(BF16)
                tiles += [jnp.where(g, value, none[:HEADS]) for g in hot]
            first.append(jnp.concatenate(tiles, 0))
            second.append(jnp.where(spread(low_key, q, r, LOW).astype(BF16) == lows, ones, none))
        total = lax.dot_general(
            jnp.concatenate(first, 1),
            jnp.concatenate(second, 1),
            (((1,), (1,)), ((), ())),
            preferred_element_type=F32,
        )
        sums_ref[r] = jnp.where(fresh, total, total + sums_ref[r])

    both = (stages[:6], stages[6:])

    def work(chunk, stage_in, stage_out, fresh=None):
        done = 0
        for q in range(per):
            until = (q + 1) * rows // per
            if stage_out is not None:
                for r in range(done, until):
                    bin_row(r, stage_out, fresh)
            if stage_in is not None:
                level(chunk, q, stage_in)
            done = until

    for copy in copies_in(0):
        copy.wait()
    work(0, both[0], None)
    copy_out(0).start()

    def pair(i, carry):
        for copy in copies_in(i + 1):
            copy.wait()
        for j in range(size // per):
            work(2 * i + 1 + j, both[(1 + j) % 2], both[j % 2], 2 * i + j == 0)
        copy_out(i + 1).start()
        return carry

    lax.fori_loop(0, pieces - 1, pair, 0)
    work(0, None, both[(chunks - 1) % 2], place_ref[0] < 0)
    running = jnp.zeros((HEADS, LOW), F32)
    for r in range(rows):
        tiles = [sums_ref[r, pl.ds(i * half, half)] for i in range(8)]
        joined = [tiles[2 * i] + tiles[2 * i + 1] for i in range(4)]
        flow = jnp.concatenate(joined[:2], 0)
        running = running + jnp.concatenate(joined[2:], 0)
        share_ref[r] = jnp.concatenate([flow, running], 1)
    for d in range(parts):
        owner = place_ref[d]
        piece_refs[d][0:share] = share_ref[pl.ds(owner * share, share)]
        piece_refs[d][share] = share_ref[rows - 1]
    for piece in range(pieces):
        copy_out(piece).wait()


def step_and_bin(parts, place, thick, depth, basins, edges, fields):
    levels, rows, cols = fields[0].shape
    per = next(n for n in range(PER, 0, -1) if levels % n == 0)
    pieces = 1 + levels // per // 2
    halves = cols // LANES
    tall = edges[2].shape[1]
    share = rows // parts

    def vmem(shape, dtype=F32):
        return pltpu.VMEM(shape, dtype)

    whole = vmem((levels, rows, cols))
    compact = vmem((rows, LANES))
    piece = (share + 1, HEADS, 2 * LOW)
    return pl.pallas_call(
        main_kernel,
        in_specs=[pl.BlockSpec(memory_space=pltpu.SMEM)] * 2
        + [pl.BlockSpec(memory_space=pltpu.VMEM)] * 10
        + [pl.BlockSpec(memory_space=pl.ANY)] * 4,
        out_specs=[pl.BlockSpec(memory_space=pl.ANY)] + [pl.BlockSpec(memory_space=pltpu.VMEM)] * parts,
        out_shape=[jax.ShapeDtypeStruct((levels, rows, cols), F32)] + [jax.ShapeDtypeStruct(piece, F32)] * parts,
        scratch_shapes=[
            whole, whole, whole, vmem((levels, rows, cols), jnp.int32), whole,
            pltpu.SemaphoreType.DMA((pieces, 4)),
            pltpu.SemaphoreType.DMA((pieces,)),
            vmem((rows, cols), jnp.int32),
            vmem((rows, cols), jnp.int32),
            vmem((rows, cols), jnp.int32),
            compact, compact, compact, compact,
            vmem((tall, cols)),
            vmem((tall, cols)),
            vmem((rows, 4 * HEADS, LOW)),
            vmem((per, halves, 3, rows + 16, LANES)),
            vmem((rows, HEADS, 2 * LOW)),
        ]
        + [vmem((per, rows, cols))] * 12,
        compiler_params=pltpu.CompilerParams(vmem_limit_bytes=VMEM),
        name="step_and_bin",
    )(place, thick, depth, basins, *edges, *fields)


def close_kernel(scales, pieces, *refs):
    piece_refs, carry_refs = (refs[:pieces], refs[pieces:-4])
    over_ref, tend_ref, up_ref, run_ref = refs[-4:]
    share = piece_refs[0].shape[0] - 1
    total = piece_refs[0][0:share]
    for ref in piece_refs[1:]:
        total = total + ref[0:share]
    total = total.reshape(share * HEADS, 2 * LOW)
    source = row_ids((2 * LOW, 2 * LOW))
    target = lane_ids((2 * LOW, 2 * LOW))
    after = (source < LOW) & ((target >= LOW) | (source >= target))
    up_ref[...] = jnp.dot(total, after.astype(F32), precision=lax.Precision.HIGHEST, preferred_element_type=F32)
    run_ref[...] = total
    carry = jnp.zeros((HEADS, 2 * LOW), F32)
    for ref in carry_refs:
        carry = carry + ref[...]
    for b in range(B):
        above = jnp.zeros((share, LOW), F32)
        for high in reversed(range(HIGH)):
            head = b * HIGH + high
            rows = up_ref[pl.ds(head, share, HEADS), :]
            over_ref[b, :, high * LOW : (high + 1) * LOW] = (rows[:, :LOW] + above) * scales[0]
            above = above + rows[:, LOW:]
            rows = run_ref[pl.ds(head, share, HEADS), :] + carry[head : head + 1]
            tend_ref[b, :, high * LOW : (high + 1) * LOW] = rows[:, LOW:] * scales[1]


def close(pieces, carries, scales):
    share = pieces[0].shape[0] - 1
    out = jax.ShapeDtypeStruct((B, share, C), F32)
    scratch = pltpu.VMEM((share * HEADS, 2 * LOW), F32)
    return pl.pallas_call(
        functools.partial(close_kernel, scales, len(pieces)),
        out_shape=[out, out],
        scratch_shapes=[scratch, scratch],
        name="close_sums",
    )(*pieces, *carries)


def body(tracer, u_flow, v_flow, depth_levels, class_index, basin_index, level_thickness):
    levels, rows, cols = tracer.shape
    lons, lats = (lax.axis_size("lon"), lax.axis_size("lat"))
    here = lax.axis_index("lon")

    def ahead(count):
        return [(i, i + 1) for i in range(count - 1)]

    def behind(count):
        return [(i + 1, i) for i in range(count - 1)]

    right, left, up, down = pack(tracer, u_flow, v_flow, depth_levels)
    west = lax.ppermute(right, "lon", ahead(lons))
    far = lax.ppermute(left, "lon", behind(lons))
    south = lax.ppermute(up, "lat", ahead(lats))
    north = lax.ppermute(down, "lat", behind(lats))
    place = (here + jnp.arange(lons, dtype=jnp.int32)) % lons
    tracer_next, *pieces = step_and_bin(
        lons,
        place,
        level_thickness,
        depth_levels,
        basin_index,
        (right, left, up, down, west, far, south, north),
        (tracer, u_flow, v_flow, class_index),
    )
    pieces = pieces[:1] + [
        lax.ppermute(pieces[d], "lon", [(i, (i + d) % lons) for i in range(lons)]) for d in range(1, lons)
    ]
    share = rows // lons
    block_total = sum(p[share] for p in pieces)
    carries = [lax.ppermute(block_total, "lat", [(i, i + d) for i in range(lats - d)]) for d in range(1, lats)]
    unit = 1.0 / math.sqrt(cols * lons * levels)
    overturning, tendency = close(pieces, carries, (16.0 * unit, 4.0 * unit))
    return (tracer_next, overturning, tendency)


def solution(mesh):
    return jax.shard_map(
        body,
        mesh=mesh,
        in_specs=(
            P("member", "lat", "lon"),
            P("member", "lat", "lon"),
            P("member", "lat", "lon"),
            P(("member", "lat"), "lon"),
            P("member", "lat", "lon"),
            P(("member", "lat"), "lon"),
            P(),
        ),
        out_specs=(
            P("member", "lat", "lon"),
            P("member", ("lat", "lon"), None),
            P("member", ("lat", "lon"), None),
        ),
        check_vma=False,
    )
```

```python
import functools
import math

import jax
import jax.numpy as jnp
from jax import lax
from jax.experimental import pallas as pl
from jax.experimental.pallas import tpu as pltpu
from jax.sharding import PartitionSpec as P

C = 192
B = 5
DIFFUSION = 0.1

LANES = 128
LOW = 64
HIGH = C // LOW
HEADS = 16
PER = 5
SLOTS = 5
VMEM = 63 << 20
F32 = jnp.float32
BF16 = jnp.bfloat16


def lane_ids(shape):
    return lax.broadcasted_iota(jnp.int32, shape, len(shape) - 1)


def row_ids(shape):
    return lax.broadcasted_iota(jnp.int32, shape, len(shape) - 2)


def flux_of(here, slope, bend, bend_ahead, speed):
    value = here + 0.5 * slope - jnp.where(speed > 0.0, bend, bend_ahead)
    return speed * value - DIFFUSION * slope


def sixth(behind, here, ahead):
    return ((ahead - here) - (here - behind)) * (1.0 / 6.0)


def rows_kernel(south_ref, north_ref, speed_ref, depth_ref, up_ref, down_ref):
    levels = south_ref.shape[0]
    rows = depth_ref.shape[0]

    def level(k, carry):
        here = pl.ds(k, 1)
        lower = jnp.where(k < depth_ref[0:8], south_ref[k], 0.0)
        upper = jnp.where(k < depth_ref[rows - 8 :], north_ref[k], 0.0)
        up_ref[0, here, :] = upper[6:7]
        up_ref[1, here, :] = upper[7:8]
        up_ref[2, here, :] = speed_ref[k, 7:8, :]
        down_ref[0, here, :] = lower[0:1]
        down_ref[1, here, :] = lower[1:2]
        return carry

    lax.fori_loop(0, levels, level, 0, unroll=15)
    up_ref[0, levels : levels + 1, :] = depth_ref[rows - 1 : rows].astype(F32)
    down_ref[0, levels : levels + 1, :] = depth_ref[0:1].astype(F32)


def pack_rows(tracer, v_flow, depth):
    levels, rows, cols = tracer.shape
    tall = (levels + 8) // 8 * 8
    shapes = [(3, tall, cols), (2, tall, cols)]
    return pl.pallas_call(
        rows_kernel,
        grid=(1,),
        in_specs=[
            pl.BlockSpec((levels, 8, cols), lambda i: (0, 0, 0)),
            pl.BlockSpec((levels, 8, cols), lambda i: (0, rows // 8 - 1, 0)),
            pl.BlockSpec((levels, 8, cols), lambda i: (0, rows // 8 - 1, 0)),
            pl.BlockSpec((rows, cols), lambda i: (0, 0)),
        ],
        out_specs=[pl.BlockSpec(s, lambda i: (0, 0, 0)) for s in shapes],
        out_shape=[jax.ShapeDtypeStruct(s, F32) for s in shapes],
        compiler_params=pltpu.CompilerParams(vmem_limit_bytes=VMEM),
        name="pack_rows",
    )(tracer, tracer, v_flow, depth)


def columns_kernel(tracer_ref, east_ref, depth_ref, side_ref):
    per, rows, cols = tracer_ref.shape
    step = pl.program_id(0)
    lanes = lane_ids((rows, LANES))
    owner, slot = (lanes // SLOTS, lanes % SLOTS)
    depth = depth_ref[...]
    near, away = (depth[:, :LANES], depth[:, cols - LANES :])
    deep = jnp.where(lanes < LANES // 2, near, away)
    value = pltpu.roll(deep.astype(F32), SLOTS * per + 2, 1)
    for q in range(per):
        k = step * per + q
        ends = jnp.where(lanes < LANES // 2, tracer_ref[q, :, :LANES], tracer_ref[q, :, cols - LANES :])
        turned = pltpu.roll(jnp.where(k < deep, ends, 0.0), SLOTS * q + 2, 1)
        turned = jnp.where(slot == SLOTS - 1, pltpu.roll(east_ref[q], SLOTS * q + SLOTS, 1), turned)
        value = jnp.where(owner == q, turned, value)
    side_ref[:, pl.ds(pl.multiple_of(step * LANES, LANES), LANES)] = value


def levels_of_tile(levels):
    return next(n for n in range((LANES - 3) // SLOTS, 0, -1) if levels % n == 0)


def pack_columns(tracer, u_flow, depth):
    levels, rows, cols = tracer.shape
    per = levels_of_tile(levels)
    tiles = levels // per
    return pl.pallas_call(
        columns_kernel,
        grid=(tiles,),
        in_specs=[
            pl.BlockSpec((per, rows, cols), lambda i: (i, 0, 0)),
            pl.BlockSpec((per, rows, LANES), lambda i: (i, 0, cols // LANES - 1)),
            pl.BlockSpec((rows, cols), lambda i: (0, 0)),
        ],
        out_specs=pl.BlockSpec((rows, tiles * LANES), lambda i: (0, 0)),
        out_shape=jax.ShapeDtypeStruct((rows, tiles * LANES), F32),
        compiler_params=pltpu.CompilerParams(vmem_limit_bytes=VMEM),
        name="pack_columns",
    )(tracer, u_flow, depth)


def main_kernel(
    thick_ref, depth_ref, basin_ref, side_ref, up_ref, down_ref,
    west_hbm, far_hbm, south_hbm, ahead_hbm, tracer_hbm, east_hbm, north_hbm, class_hbm,
    *refs,
):
    scratch = 26 + 12
    next_hbm, total_ref, *piece_refs = refs[: len(refs) - scratch]
    (
        tracer_ref, east_ref, north_ref, class_ref, next_ref, in_sem, out_sem, halo_sem,
        west_ref, far_ref, south_ref, ahead_ref,
        head_ref, zonal_ref, merid_ref, far_value, far_bend, west_slope, west_flux,
        ahead_value, ahead_bend, south_value, south_flux,
        sums_ref, tall_ref, share_ref,
    ) = refs[len(refs) - scratch : len(refs) - 12]
    stages = refs[len(refs) - 12 :]
    levels, rows, cols = tracer_ref.shape
    halves = cols // LANES
    per = stages[0].shape[0]
    chunks = levels // per
    parts = len(piece_refs)
    share = rows // parts
    place = lax.axis_index("lon")
    lat = lax.axis_index("lat")

    bounds = [(0, per)] + [(per * (2 * i + 1), min(2 * per, levels - per * (2 * i + 1))) for i in range(chunks // 2)]
    size = {n for _, n in bounds[1:]}
    assert len(size) == 1
    size = size.pop()

    def span(piece):
        if isinstance(piece, int) and piece == 0:
            return pl.ds(0, per)
        return pl.ds(per + (piece - 1) * size, size)

    sources = ((tracer_hbm, tracer_ref), (east_hbm, east_ref), (north_hbm, north_ref), (class_hbm, class_ref))
    halos = ((west_hbm, west_ref), (far_hbm, far_ref), (south_hbm, south_ref), (ahead_hbm, ahead_ref))

    def copies_in(piece):
        return [
            pltpu.make_async_copy(src.at[span(piece)], dst.at[span(piece)], in_sem.at[piece, i])
            for i, (src, dst) in enumerate(sources)
        ]

    def copy_out(piece):
        return pltpu.make_async_copy(next_ref.at[span(piece)], next_hbm.at[span(piece)], out_sem.at[piece])

    pieces = len(bounds)
    edges = [pltpu.make_async_copy(src, dst, halo_sem.at[i]) for i, (src, dst) in enumerate(halos)]
    for copy in edges:
        copy.start()
    for piece in range(pieces):
        for copy in copies_in(piece):
            copy.start()
    for copy in edges:
        copy.wait()

    span_of = levels_of_tile(levels)
    tiles = levels // span_of
    lanes = lane_ids((rows, LANES))
    slots = lanes % SLOTS
    depth = depth_ref[...].astype(F32)
    has_west, has_far = (place > 0, place < parts - 1)
    for tile in range(tiles):
        part = slice(tile * LANES, (tile + 1) * LANES)
        own = side_ref[:, part]
        west = jnp.where(has_west, west_ref[:, part], 0.0)
        far = jnp.where(has_far, far_ref[:, part], 0.0)
        speed = pltpu.roll(west, LANES - SLOTS + 2, 1)

        def beside(x):
            return pltpu.roll(x, LANES - 1, 1)

        def curve(x):
            return sixth(pltpu.roll(x, 1, 1), x, beside(x))

        right = jnp.where(slots < 2, own, far)
        far_value[:, part] = right
        far_bend[:, part] = curve(right)
        left = jnp.where(slots < 2, west, own)
        slope = beside(left) - left
        west_slope[:, part] = slope
        bend = curve(left)
        flux = flux_of(left, slope, bend, beside(bend), speed)
        lane = SLOTS * span_of
        faces = jnp.minimum(west[:, lane + 1 : lane + 2], depth[:, :1])
        west_flux[:, part] = jnp.where((lanes // SLOTS + tile * span_of).astype(F32) < faces, flux, 0.0)
        if tile == 0:
            wide = lane_ids((rows, cols))
            after = jnp.where(wide == cols - 1, far[:, lane + 2 : lane + 3], pltpu.roll(depth, cols - 1, 1))
            zonal_ref[...] = jnp.minimum(depth, after).astype(jnp.int32)

    has_south, has_ahead = (lat > 0, lat < lax.axis_size("lat") - 1)
    first, second = (down_ref[0], down_ref[1])
    here = jnp.where(has_south, south_ref[1], 0.0)
    behind = jnp.where(has_south, south_ref[0], 0.0)
    speed = jnp.where(has_south, south_ref[2], 0.0)
    beyond = jnp.where(has_ahead, ahead_ref[0], 0.0)
    south_value[...] = here
    ahead_value[...] = beyond
    ahead_bend[...] = sixth(up_ref[1], beyond, jnp.where(has_ahead, ahead_ref[1], 0.0))
    flux = flux_of(here, first - here, sixth(behind, here, first), sixth(here, first, second), speed)
    faces = jnp.minimum(behind[levels : levels + 1, :], depth[0:1])
    south_flux[...] = jnp.where(row_ids(flux.shape).astype(F32) < faces, flux, 0.0)
    above = pltpu.roll(depth, rows - 1, 0)
    above = jnp.where(row_ids((rows, cols)) == rows - 1, beyond[levels : levels + 1, :], above)
    merid_ref[...] = jnp.minimum(depth, above).astype(jnp.int32)
    head_ref[...] = basin_ref[...] * HIGH

    top = 8
    inner = pl.ds(top, rows)

    def level(chunk, q, stage):
        flow_hi, flow_lo, gain_hi, gain_lo, head_key, low_key = stage
        k = chunk * per + q
        thick = thick_ref[k]
        here = pl.ds(k, 1)
        edge = lane_ids((rows, LANES))
        at_end, at_start = (edge == LANES - 1, edge == 0)

        def split(array):
            return [array[:, h * LANES : (h + 1) * LANES] for h in range(halves)]

        def turn_back(blocks, outside):
            turned = [pltpu.roll(x, LANES - 1, 1) for x in blocks] + [outside]
            return [jnp.where(at_end, turned[h + 1], turned[h]) for h in range(halves)]

        def turn_on(blocks, outside):
            turned = [outside] + [pltpu.roll(x, 1, 1) for x in blocks]
            return [jnp.where(at_start, turned[h], turned[h + 1]) for h in range(halves)]

        tile = pl.ds(pl.multiple_of(k // span_of * LANES, LANES), LANES)
        slot = SLOTS * (k % span_of)

        def to_end(ref):
            return pltpu.roll(ref[:, tile], LANES - 3 - slot, 1)

        def to_start(ref):
            return pltpu.roll(ref[:, tile], LANES - 1 - slot, 1)

        depth = split(depth_ref[...])
        raw = split(tracer_ref[k])
        wet = [k < d for d in depth]
        masked = [jnp.where(w, x, 0.0) for w, x in zip(wet, raw)]

        ahead = turn_back(masked, to_end(far_value))
        slope = [a - x for a, x in zip(ahead, masked)]
        slope_behind = turn_on(slope, to_start(west_slope))
        bend = [(a - b) * (1.0 / 6.0) for a, b in zip(slope, slope_behind)]
        bend_ahead = turn_back(bend, to_end(far_bend))
        speed = split(east_ref[k])
        shut = [k >= d for d in split(zonal_ref[...])]
        flux = [
            jnp.where(s, 0.0, flux_of(*x)) for s, *x in zip(shut, masked, slope, bend, bend_ahead, speed)
        ]
        flux_behind = turn_on(flux, to_start(west_flux))
        left_over = [m - (a - b) for m, a, b in zip(masked, flux, flux_behind)]

        north = split(north_ref[k])
        shut = [k >= d for d in split(merid_ref[...])]
        classes = split(class_ref[k])
        heads = split(head_ref[...])
        below, over = (split(south_value[here, :]), split(ahead_value[here, :]))
        over_bend, below_flux = (split(ahead_bend[here, :]), split(south_flux[here, :]))
        for h in range(halves):
            part = slice(h * LANES, (h + 1) * LANES)
            rows_of = tall_ref.at[q, h]
            rows_of[0, inner, :] = masked[h]
            rows_of[0, top - 1 : top, :] = below[h]
            rows_of[0, top + rows : top + rows + 1, :] = over[h]
            slope = rows_of[0, pl.ds(top + 1, rows), :] - masked[h]
            slope_behind = masked[h] - rows_of[0, pl.ds(top - 1, rows), :]
            bend = (slope - slope_behind) * (1.0 / 6.0)
            rows_of[1, inner, :] = bend
            rows_of[1, top + rows : top + rows + 1, :] = over_bend[h]
            bend_ahead = rows_of[1, pl.ds(top + 1, rows), :]
            flux = jnp.where(shut[h], 0.0, flux_of(masked[h], slope, bend, bend_ahead, north[h]))
            rows_of[2, inner, :] = flux
            rows_of[2, top - 1 : top, :] = below_flux[h]
            flux_behind = rows_of[2, pl.ds(top - 1, rows), :]
            updated = jnp.where(wet[h], left_over[h] - (flux - flux_behind), 0.0)
            next_ref[k, :, part] = updated
            flow = jnp.where(shut[h], 0.0, north[h] * thick)
            gain = (updated - masked[h]) * thick
            upper = flow.astype(BF16).astype(F32)
            flow_hi[q, :, part] = flow
            flow_lo[q, :, part] = flow - upper
            upper = gain.astype(BF16).astype(F32)
            gain_hi[q, :, part] = gain
            gain_lo[q, :, part] = gain - upper
            head_key[q, :, part] = (heads[h] + (classes[h] >> 6)).astype(F32)
            low_key[q, :, part] = (classes[h] & (LOW - 1)).astype(F32)

    half = HEADS // 2
    order = row_ids((HEADS, cols))
    heads = [(order % half + g * half).astype(F32).astype(BF16) for g in range(2)]
    lows = row_ids((LOW, cols)).astype(F32).astype(BF16)
    ones = jnp.ones((LOW, cols), BF16)
    none = jnp.zeros((LOW, cols), BF16)

    def spread(ref, q, r, count):
        return jnp.broadcast_to(ref[q, r : r + 1, :], (count, cols))

    def bin_row(r, stage, fresh):
        *terms, head_key, low_key = stage
        first, second = ([], [])
        for q in range(per):
            key = spread(head_key, q, r, HEADS).astype(BF16)
            hot = [key == g for g in heads]
            tiles = []
            for upper, lower in (terms[:2], terms[2:]):
                value = jnp.concatenate([spread(upper, q, r, half), spread(lower, q, r, half)], 0).astype(BF16)
                tiles += [jnp.where(g, value, none[:HEADS]) for g in hot]
            first.append(jnp.concatenate(tiles, 0))
            second.append(jnp.where(spread(low_key, q, r, LOW).astype(BF16) == lows, ones, none))
        total = lax.dot_general(
            jnp.concatenate(first, 1),
            jnp.concatenate(second, 1),
            (((1,), (1,)), ((), ())),
            preferred_element_type=F32,
        )
        sums_ref[r] = jnp.where(fresh, total, total + sums_ref[r])

    both = (stages[:6], stages[6:])

    def work(chunk, stage_in, stage_out, fresh=None):
        done = 0
        for q in range(per):
            until = (q + 1) * rows // per
            if stage_out is not None:
                for r in range(done, until):
                    bin_row(r, stage_out, fresh)
            if stage_in is not None:
                level(chunk, q, stage_in)
            done = until

    for copy in copies_in(0):
        copy.wait()
    work(0, both[0], None)
    copy_out(0).start()

    def pair(i, carry):
        for copy in copies_in(i + 1):
            copy.wait()
        for j in range(size // per):
            work(2 * i + 1 + j, both[(1 + j) % 2], both[j % 2], 2 * i + j == 0)
        copy_out(i + 1).start()
        return carry

    lax.fori_loop(0, pieces - 1, pair, 0)
    work(0, None, both[(chunks - 1) % 2], place < 0)
    running = jnp.zeros((HEADS, LOW), F32)
    for r in range(rows):
        tiles = [sums_ref[r, pl.ds(i * half, half)] for i in range(8)]
        joined = [tiles[2 * i] + tiles[2 * i + 1] for i in range(4)]
        flow = jnp.concatenate(joined[:2], 0)
        running = running + jnp.concatenate(joined[2:], 0)
        share_ref[r] = jnp.concatenate([flow, running], 1)
    for d in range(parts):
        owner = lax.rem(place + d, parts)
        piece_refs[d][...] = share_ref[pl.ds(owner * share, share)]
    total_ref[...] = share_ref[rows - 1]
    for piece in range(pieces):
        copy_out(piece).wait()


def step_and_bin(parts, thick, depth, basins, edges, fields):
    levels, rows, cols = fields[0].shape
    per = next(n for n in range(PER, 0, -1) if levels % n == 0)
    pieces = 1 + levels // per // 2
    halves = cols // LANES
    tall = edges[1].shape[1]
    share = rows // parts

    def vmem(shape, dtype=F32):
        return pltpu.VMEM(shape, dtype)

    whole = vmem((levels, rows, cols))
    compact = vmem((rows, levels // levels_of_tile(levels) * LANES))
    row = vmem((tall, cols))
    level = vmem((rows, cols), jnp.int32)
    piece = (share, HEADS, 2 * LOW)
    return pl.pallas_call(
        main_kernel,
        in_specs=[pl.BlockSpec(memory_space=pltpu.SMEM)]
        + [pl.BlockSpec(memory_space=pltpu.VMEM)] * 5
        + [pl.BlockSpec(memory_space=pl.ANY)] * 8,
        out_specs=[pl.BlockSpec(memory_space=pl.ANY)] + [pl.BlockSpec(memory_space=pltpu.VMEM)] * (parts + 1),
        out_shape=[jax.ShapeDtypeStruct(s, F32) for s in [(levels, rows, cols), piece[1:]] + [piece] * parts],
        scratch_shapes=[
            whole, whole, whole, vmem((levels, rows, cols), jnp.int32), whole,
            pltpu.SemaphoreType.DMA((pieces, 4)),
            pltpu.SemaphoreType.DMA((pieces,)),
            pltpu.SemaphoreType.DMA((4,)),
        ]
        + [vmem(edge.shape) for edge in edges[3:]]
        + [
            level, level, level,
            compact, compact, compact, compact,
            row, row, row, row,
            vmem((rows, 4 * HEADS, LOW)),
            vmem((per, halves, 3, rows + 16, LANES)),
            vmem((rows, HEADS, 2 * LOW)),
        ]
        + [vmem((per, rows, cols))] * 12,
        compiler_params=pltpu.CompilerParams(vmem_limit_bytes=VMEM),
        name="step_and_bin",
    )(thick, depth, basins, *edges, *fields)


def close_kernel(scales, pieces, carries, *refs):
    count = pieces + carries
    sources, (over_ref, tend_ref), landed = (refs[:count], refs[count : count + 2], refs[count + 2 : 2 * count + 2])
    up_ref, run_ref, sem = refs[2 * count + 2 :]
    copies = [pltpu.make_async_copy(src, dst, sem.at[i]) for i, (src, dst) in enumerate(zip(sources, landed))]
    for copy in copies:
        copy.start()
    source = row_ids((2 * LOW, 2 * LOW))
    target = lane_ids((2 * LOW, 2 * LOW))
    after = ((source < LOW) & ((target >= LOW) | (source >= target))).astype(F32)
    for copy in copies:
        copy.wait()
    piece_refs, carry_refs = (landed[:pieces], landed[pieces:])
    share = piece_refs[0].shape[0]
    total = piece_refs[0][...]
    for ref in piece_refs[1:]:
        total = total + ref[...]
    total = total.reshape(share * HEADS, 2 * LOW)
    up_ref[...] = jnp.dot(total, after, precision=lax.Precision.HIGHEST, preferred_element_type=F32)
    run_ref[...] = total
    carry = jnp.zeros((HEADS, 2 * LOW), F32)
    for ref in carry_refs:
        carry = carry + ref[...]
    for b in range(B):
        above = jnp.zeros((share, LOW), F32)
        for high in reversed(range(HIGH)):
            head = b * HIGH + high
            rows = up_ref[pl.ds(head, share, HEADS), :]
            over_ref[b, :, high * LOW : (high + 1) * LOW] = (rows[:, :LOW] + above) * scales[0]
            above = above + rows[:, LOW:]
            rows = run_ref[pl.ds(head, share, HEADS), :] + carry[head : head + 1]
            tend_ref[b, :, high * LOW : (high + 1) * LOW] = rows[:, LOW:] * scales[1]


def close(pieces, carries, scales):
    share = pieces[0].shape[0]
    out = jax.ShapeDtypeStruct((B, share, C), F32)
    inputs = (*pieces, *carries)
    scratch = pltpu.VMEM((share * HEADS, 2 * LOW), F32)
    return pl.pallas_call(
        functools.partial(close_kernel, scales, len(pieces), len(carries)),
        in_specs=[pl.BlockSpec(memory_space=pl.ANY)] * len(inputs),
        out_shape=[out, out],
        scratch_shapes=[pltpu.VMEM(x.shape, F32) for x in inputs]
        + [scratch, scratch, pltpu.SemaphoreType.DMA((len(inputs),))],
        compiler_params=pltpu.CompilerParams(vmem_limit_bytes=VMEM),
        name="close_sums",
    )(*inputs)


def turn(count, step):
    return [(i, (i + step) % count) for i in range(count)]


def body(tracer, u_flow, v_flow, depth_levels, class_index, basin_index, level_thickness):
    levels, rows, cols = tracer.shape
    lons, lats = (lax.axis_size("lon"), lax.axis_size("lat"))
    up, down = pack_rows(tracer, v_flow, depth_levels)
    south = lax.ppermute(up, "lat", turn(lats, 1))
    ahead = lax.ppermute(down, "lat", turn(lats, -1))
    side = pack_columns(tracer, u_flow, depth_levels)
    west = lax.ppermute(side, "lon", turn(lons, 1))
    far = lax.ppermute(side, "lon", turn(lons, -1))
    tracer_next, block_total, *pieces = step_and_bin(
        lons,
        level_thickness,
        depth_levels,
        basin_index,
        (side, up, down, west, far, south, ahead),
        (tracer, u_flow, v_flow, class_index),
    )
    pieces = pieces[:1] + [lax.ppermute(pieces[d], "lon", turn(lons, d)) for d in range(1, lons)]
    lat = lax.axis_index("lat")
    carry = jnp.zeros((HEADS, 2 * LOW), F32)
    for d in range(1, lats):
        carry = carry + jnp.where(lat >= d, lax.ppermute(block_total, "lat", turn(lats, d)), 0.0)
    carries = [carry] + [lax.ppermute(carry, "lon", turn(lons, d)) for d in range(1, lons)]
    unit = 1.0 / math.sqrt(cols * lons * levels)
    overturning, tendency = close(pieces, carries, (16.0 * unit, 4.0 * unit))
    return (tracer_next, overturning, tendency)


def solution(mesh):
    return jax.shard_map(
        body,
        mesh=mesh,
        in_specs=(
            P("member", "lat", "lon"),
            P("member", "lat", "lon"),
            P("member", "lat", "lon"),
            P(("member", "lat"), "lon"),
            P("member", "lat", "lon"),
            P(("member", "lat"), "lon"),
            P(),
        ),
        out_specs=(
            P("member", "lat", "lon"),
            P("member", ("lat", "lon"), None),
            P("member", ("lat", "lon"), None),
        ),
        check_vma=False,
    )
```

```python
import functools
import math

import jax
import jax.numpy as jnp
from jax import lax
from jax.experimental import pallas as pl
from jax.experimental.pallas import tpu as pltpu
from jax.sharding import PartitionSpec as P

C = 192
B = 5
DIFFUSION = 0.1

LANES = 128
LOW = 64
HIGH = C // LOW
HEADS = 16
PER = 5
SLOTS = 5
VMEM = 64 << 20
F32 = jnp.float32
BF16 = jnp.bfloat16


def lane_ids(shape):
    return lax.broadcasted_iota(jnp.int32, shape, len(shape) - 1)


def row_ids(shape):
    return lax.broadcasted_iota(jnp.int32, shape, len(shape) - 2)


def flux_of(here, slope, bend, bend_ahead, speed):
    value = here + 0.5 * slope - jnp.where(speed > 0.0, bend, bend_ahead)
    return speed * value - DIFFUSION * slope


def sixth(behind, here, ahead):
    return ((ahead - here) - (here - behind)) * (1.0 / 6.0)


def rows_kernel(south_ref, north_ref, speed_ref, depth_ref, up_ref, down_ref):
    levels = south_ref.shape[0]
    rows = depth_ref.shape[0]

    def level(k, carry):
        here = pl.ds(k, 1)
        lower = jnp.where(k < depth_ref[0:8], south_ref[k], 0.0)
        upper = jnp.where(k < depth_ref[rows - 8 :], north_ref[k], 0.0)
        up_ref[0, here, :] = upper[6:7]
        up_ref[1, here, :] = upper[7:8]
        up_ref[2, here, :] = speed_ref[k, 7:8, :]
        down_ref[0, here, :] = lower[0:1]
        down_ref[1, here, :] = lower[1:2]
        return carry

    lax.fori_loop(0, levels, level, 0, unroll=15)
    up_ref[0, levels : levels + 1, :] = depth_ref[rows - 1 : rows].astype(F32)
    down_ref[0, levels : levels + 1, :] = depth_ref[0:1].astype(F32)


def pack_rows(tracer, v_flow, depth):
    levels, rows, cols = tracer.shape
    tall = (levels + 8) // 8 * 8
    shapes = [(3, tall, cols), (2, tall, cols)]
    return pl.pallas_call(
        rows_kernel,
        grid=(1,),
        in_specs=[
            pl.BlockSpec((levels, 8, cols), lambda i: (0, 0, 0)),
            pl.BlockSpec((levels, 8, cols), lambda i: (0, rows // 8 - 1, 0)),
            pl.BlockSpec((levels, 8, cols), lambda i: (0, rows // 8 - 1, 0)),
            pl.BlockSpec((rows, cols), lambda i: (0, 0)),
        ],
        out_specs=[pl.BlockSpec(s, lambda i: (0, 0, 0)) for s in shapes],
        out_shape=[jax.ShapeDtypeStruct(s, F32) for s in shapes],
        compiler_params=pltpu.CompilerParams(vmem_limit_bytes=VMEM),
        name="pack_rows",
    )(tracer, tracer, v_flow, depth)


def columns_kernel(tracer_ref, east_ref, depth_ref, side_ref):
    per, rows, cols = tracer_ref.shape
    step = pl.program_id(0)
    lanes = lane_ids((rows, LANES))
    owner, slot = (lanes // SLOTS, lanes % SLOTS)
    depth = depth_ref[...]
    near, away = (depth[:, :LANES], depth[:, cols - LANES :])
    deep = jnp.where(lanes < LANES // 2, near, away)
    value = pltpu.roll(deep.astype(F32), SLOTS * per + 2, 1)
    for q in range(per):
        k = step * per + q
        ends = jnp.where(lanes < LANES // 2, tracer_ref[q, :, :LANES], tracer_ref[q, :, cols - LANES :])
        turned = pltpu.roll(jnp.where(k < deep, ends, 0.0), SLOTS * q + 2, 1)
        turned = jnp.where(slot == SLOTS - 1, pltpu.roll(east_ref[q], SLOTS * q + SLOTS, 1), turned)
        value = jnp.where(owner == q, turned, value)
    side_ref[:, pl.ds(pl.multiple_of(step * LANES, LANES), LANES)] = value


def levels_of_tile(levels):
    return next(n for n in range((LANES - 3) // SLOTS, 0, -1) if levels % n == 0)


def pack_columns(tracer, u_flow, depth):
    levels, rows, cols = tracer.shape
    per = levels_of_tile(levels)
    tiles = levels // per
    return pl.pallas_call(
        columns_kernel,
        grid=(tiles,),
        in_specs=[
            pl.BlockSpec((per, rows, cols), lambda i: (i, 0, 0)),
            pl.BlockSpec((per, rows, LANES), lambda i: (i, 0, cols // LANES - 1)),
            pl.BlockSpec((rows, cols), lambda i: (0, 0)),
        ],
        out_specs=pl.BlockSpec((rows, tiles * LANES), lambda i: (0, 0)),
        out_shape=jax.ShapeDtypeStruct((rows, tiles * LANES), F32),
        compiler_params=pltpu.CompilerParams(vmem_limit_bytes=VMEM),
        name="pack_columns",
    )(tracer, u_flow, depth)


def main_kernel(
    thick_ref, depth_ref, basin_ref, side_ref, up_ref, down_ref,
    west_hbm, far_hbm, south_hbm, ahead_hbm, tracer_hbm, east_hbm, north_hbm, class_hbm,
    *refs,
):
    scratch = 26 + 12
    next_hbm, total_ref, *piece_refs = refs[: len(refs) - scratch]
    (
        tracer_ref, east_ref, north_ref, class_ref, next_ref, in_sem, out_sem, halo_sem,
        west_ref, far_ref, south_ref, ahead_ref,
        head_ref, zonal_ref, merid_ref, far_value, far_bend, west_slope, west_flux,
        ahead_value, ahead_bend, south_value, south_flux,
        sums_ref, tall_ref, share_ref,
    ) = refs[len(refs) - scratch : len(refs) - 12]
    stages = refs[len(refs) - 12 :]
    levels, rows, cols = tracer_ref.shape
    halves = cols // LANES
    per = stages[0].shape[0]
    chunks = levels // per
    parts = len(piece_refs)
    share = rows // parts
    place = lax.axis_index("lon")
    lat = lax.axis_index("lat")

    bounds = [(0, per)] + [(per * (2 * i + 1), min(2 * per, levels - per * (2 * i + 1))) for i in range(chunks // 2)]
    size = {n for _, n in bounds[1:]}
    assert len(size) == 1
    size = size.pop()

    def span(piece):
        if isinstance(piece, int) and piece == 0:
            return pl.ds(0, per)
        return pl.ds(per + (piece - 1) * size, size)

    sources = ((tracer_hbm, tracer_ref), (east_hbm, east_ref), (north_hbm, north_ref), (class_hbm, class_ref))
    halos = ((west_hbm, west_ref), (far_hbm, far_ref), (south_hbm, south_ref), (ahead_hbm, ahead_ref))

    def copies_in(piece):
        return [
            pltpu.make_async_copy(src.at[span(piece)], dst.at[span(piece)], in_sem.at[piece, i])
            for i, (src, dst) in enumerate(sources)
        ]

    def copy_out(piece):
        return pltpu.make_async_copy(next_ref.at[span(piece)], next_hbm.at[span(piece)], out_sem.at[piece])

    pieces = len(bounds)
    edges = [pltpu.make_async_copy(src, dst, halo_sem.at[i]) for i, (src, dst) in enumerate(halos)]
    for copy in edges:
        copy.start()
    for piece in range(2):
        for copy in copies_in(piece):
            copy.start()
    for copy in edges:
        copy.wait()

    span_of = levels_of_tile(levels)
    tiles = levels // span_of
    lanes = lane_ids((rows, LANES))
    slots = lanes % SLOTS
    depth = depth_ref[...].astype(F32)
    has_west, has_far = (place > 0, place < parts - 1)
    for tile in range(tiles):
        part = slice(tile * LANES, (tile + 1) * LANES)
        own = side_ref[:, part]
        west = jnp.where(has_west, west_ref[:, part], 0.0)
        far = jnp.where(has_far, far_ref[:, part], 0.0)
        speed = pltpu.roll(west, LANES - SLOTS + 2, 1)

        def beside(x):
            return pltpu.roll(x, LANES - 1, 1)

        def curve(x):
            return sixth(pltpu.roll(x, 1, 1), x, beside(x))

        right = jnp.where(slots < 2, own, far)
        far_value[:, part] = right
        far_bend[:, part] = curve(right)
        left = jnp.where(slots < 2, west, own)
        slope = beside(left) - left
        west_slope[:, part] = slope
        bend = curve(left)
        flux = flux_of(left, slope, bend, beside(bend), speed)
        lane = SLOTS * span_of
        faces = jnp.minimum(west[:, lane + 1 : lane + 2], depth[:, :1])
        west_flux[:, part] = jnp.where((lanes // SLOTS + tile * span_of).astype(F32) < faces, flux, 0.0)
        if tile == 0:
            wide = lane_ids((rows, cols))
            after = jnp.where(wide == cols - 1, far[:, lane + 2 : lane + 3], pltpu.roll(depth, cols - 1, 1))
            zonal_ref[...] = jnp.minimum(depth, after).astype(jnp.int32)

    has_south, has_ahead = (lat > 0, lat < lax.axis_size("lat") - 1)
    first, second = (down_ref[0], down_ref[1])
    here = jnp.where(has_south, south_ref[1], 0.0)
    behind = jnp.where(has_south, south_ref[0], 0.0)
    speed = jnp.where(has_south, south_ref[2], 0.0)
    beyond = jnp.where(has_ahead, ahead_ref[0], 0.0)
    south_value[...] = here
    ahead_value[...] = beyond
    ahead_bend[...] = sixth(up_ref[1], beyond, jnp.where(has_ahead, ahead_ref[1], 0.0))
    flux = flux_of(here, first - here, sixth(behind, here, first), sixth(here, first, second), speed)
    faces = jnp.minimum(behind[levels : levels + 1, :], depth[0:1])
    south_flux[...] = jnp.where(row_ids(flux.shape).astype(F32) < faces, flux, 0.0)
    above = pltpu.roll(depth, rows - 1, 0)
    above = jnp.where(row_ids((rows, cols)) == rows - 1, beyond[levels : levels + 1, :], above)
    merid_ref[...] = jnp.minimum(depth, above).astype(jnp.int32)
    head_ref[...] = basin_ref[...] * HIGH

    top = 8
    inner = pl.ds(top, rows)

    def level(chunk, q, stage):
        flow_hi, flow_lo, gain_hi, gain_lo, head_key, low_key = stage
        k = chunk * per + q
        thick = thick_ref[k]
        here = pl.ds(k, 1)
        edge = lane_ids((rows, LANES))
        at_end, at_start = (edge == LANES - 1, edge == 0)

        def split(array):
            return [array[:, h * LANES : (h + 1) * LANES] for h in range(halves)]

        def turn_back(blocks, outside):
            turned = [pltpu.roll(x, LANES - 1, 1) for x in blocks] + [outside]
            return [jnp.where(at_end, turned[h + 1], turned[h]) for h in range(halves)]

        def turn_on(blocks, outside):
            turned = [outside] + [pltpu.roll(x, 1, 1) for x in blocks]
            return [jnp.where(at_start, turned[h], turned[h + 1]) for h in range(halves)]

        tile = pl.ds(pl.multiple_of(k // span_of * LANES, LANES), LANES)
        slot = SLOTS * (k % span_of)

        def to_end(ref):
            return pltpu.roll(ref[:, tile], LANES - 3 - slot, 1)

        def to_start(ref):
            return pltpu.roll(ref[:, tile], LANES - 1 - slot, 1)

        depth = split(depth_ref[...])
        raw = split(tracer_ref[k])
        wet = [k < d for d in depth]
        masked = [jnp.where(w, x, 0.0) for w, x in zip(wet, raw)]

        ahead = turn_back(masked, to_end(far_value))
        slope = [a - x for a, x in zip(ahead, masked)]
        slope_behind = turn_on(slope, to_start(west_slope))
        bend = [(a - b) * (1.0 / 6.0) for a, b in zip(slope, slope_behind)]
        bend_ahead = turn_back(bend, to_end(far_bend))
        speed = split(east_ref[k])
        shut = [k >= d for d in split(zonal_ref[...])]
        flux = [
            jnp.where(s, 0.0, flux_of(*x)) for s, *x in zip(shut, masked, slope, bend, bend_ahead, speed)
        ]
        flux_behind = turn_on(flux, to_start(west_flux))
        left_over = [m - (a - b) for m, a, b in zip(masked, flux, flux_behind)]

        north = split(north_ref[k])
        shut = [k >= d for d in split(merid_ref[...])]
        classes = split(class_ref[k])
        heads = split(head_ref[...])
        below, over = (split(south_value[here, :]), split(ahead_value[here, :]))
        over_bend, below_flux = (split(ahead_bend[here, :]), split(south_flux[here, :]))
        for h in range(halves):
            part = slice(h * LANES, (h + 1) * LANES)
            rows_of = tall_ref.at[q, h]
            rows_of[0, inner, :] = masked[h]
            rows_of[0, top - 1 : top, :] = below[h]
            rows_of[0, top + rows : top + rows + 1, :] = over[h]
            slope = rows_of[0, pl.ds(top + 1, rows), :] - masked[h]
            slope_behind = masked[h] - rows_of[0, pl.ds(top - 1, rows), :]
            bend = (slope - slope_behind) * (1.0 / 6.0)
            rows_of[1, inner, :] = bend
            rows_of[1, top + rows : top + rows + 1, :] = over_bend[h]
            bend_ahead = rows_of[1, pl.ds(top + 1, rows), :]
            flux = jnp.where(shut[h], 0.0, flux_of(masked[h], slope, bend, bend_ahead, north[h]))
            rows_of[2, inner, :] = flux
            rows_of[2, top - 1 : top, :] = below_flux[h]
            flux_behind = rows_of[2, pl.ds(top - 1, rows), :]
            updated = jnp.where(wet[h], left_over[h] - (flux - flux_behind), 0.0)
            next_ref[k, :, part] = updated
            flow = jnp.where(shut[h], 0.0, north[h] * thick)
            gain = (updated - masked[h]) * thick
            upper = flow.astype(BF16).astype(F32)
            flow_hi[q, :, part] = flow
            flow_lo[q, :, part] = flow - upper
            upper = gain.astype(BF16).astype(F32)
            gain_hi[q, :, part] = gain
            gain_lo[q, :, part] = gain - upper
            head_key[q, :, part] = (heads[h] + (classes[h] >> 6)).astype(F32)
            low_key[q, :, part] = (classes[h] & (LOW - 1)).astype(F32)

    half = HEADS // 2
    order = row_ids((HEADS, cols))
    heads = [(order % half + g * half).astype(F32).astype(BF16) for g in range(2)]
    lows = row_ids((LOW, cols)).astype(F32).astype(BF16)
    ones = jnp.ones((LOW, cols), BF16)
    none = jnp.zeros((LOW, cols), BF16)

    def spread(ref, q, r, count):
        return jnp.broadcast_to(ref[q, r : r + 1, :], (count, cols))

    def bin_row(r, stage, fresh):
        *terms, head_key, low_key = stage
        first, second = ([], [])
        for q in range(per):
            key = spread(head_key, q, r, HEADS).astype(BF16)
            hot = [key == g for g in heads]
            tiles = []
            for upper, lower in (terms[:2], terms[2:]):
                value = jnp.concatenate([spread(upper, q, r, half), spread(lower, q, r, half)], 0).astype(BF16)
                tiles += [jnp.where(g, value, none[:HEADS]) for g in hot]
            first.append(jnp.concatenate(tiles, 0))
            second.append(jnp.where(spread(low_key, q, r, LOW).astype(BF16) == lows, ones, none))
        total = lax.dot_general(
            jnp.concatenate(first, 1),
            jnp.concatenate(second, 1),
            (((1,), (1,)), ((), ())),
            preferred_element_type=F32,
        )
        sums_ref[r] = jnp.where(fresh, total, total + sums_ref[r])

    both = (stages[:6], stages[6:])

    def work(chunk, stage_in, stage_out, fresh=None):
        done = 0
        for q in range(per):
            until = (q + 1) * rows // per
            if stage_out is not None:
                for r in range(done, until):
                    bin_row(r, stage_out, fresh)
            if stage_in is not None:
                level(chunk, q, stage_in)
            done = until

    for copy in copies_in(0):
        copy.wait()
    work(0, both[0], None)
    copy_out(0).start()

    def pair(i, carry):
        @pl.when(i < pieces - 2)
        def _():
            for copy in copies_in(i + 2):
                copy.start()

        for copy in copies_in(i + 1):
            copy.wait()
        for j in range(size // per):
            work(2 * i + 1 + j, both[(1 + j) % 2], both[j % 2], 2 * i + j == 0)
        copy_out(i + 1).start()
        return carry

    lax.fori_loop(0, pieces - 1, pair, 0)
    work(0, None, both[(chunks - 1) % 2], place < 0)
    running = jnp.zeros((HEADS, LOW), F32)
    for r in range(rows):
        tiles = [sums_ref[r, pl.ds(i * half, half)] for i in range(8)]
        joined = [tiles[2 * i] + tiles[2 * i + 1] for i in range(4)]
        flow = jnp.concatenate(joined[:2], 0)
        running = running + jnp.concatenate(joined[2:], 0)
        share_ref[r] = jnp.concatenate([flow, running], 1)
    for d in range(parts):
        owner = lax.rem(place + d, parts)
        piece_refs[d][...] = share_ref[pl.ds(owner * share, share)]
    total_ref[...] = share_ref[rows - 1]
    for piece in range(pieces):
        copy_out(piece).wait()


def step_and_bin(parts, thick, depth, basins, edges, fields):
    levels, rows, cols = fields[0].shape
    per = next(n for n in range(PER, 0, -1) if levels % n == 0)
    pieces = 1 + levels // per // 2
    halves = cols // LANES
    tall = edges[1].shape[1]
    share = rows // parts

    def vmem(shape, dtype=F32):
        return pltpu.VMEM(shape, dtype)

    whole = vmem((levels, rows, cols))
    compact = vmem((rows, levels // levels_of_tile(levels) * LANES))
    row = vmem((tall, cols))
    level = vmem((rows, cols), jnp.int32)
    piece = (share, HEADS, 2 * LOW)
    return pl.pallas_call(
        main_kernel,
        in_specs=[pl.BlockSpec(memory_space=pltpu.SMEM)]
        + [pl.BlockSpec(memory_space=pltpu.VMEM)] * 5
        + [pl.BlockSpec(memory_space=pl.ANY)] * 8,
        out_specs=[pl.BlockSpec(memory_space=pl.ANY)] + [pl.BlockSpec(memory_space=pltpu.VMEM)] * (parts + 1),
        out_shape=[jax.ShapeDtypeStruct(s, F32) for s in [(levels, rows, cols), piece[1:]] + [piece] * parts],
        scratch_shapes=[
            whole, whole, whole, vmem((levels, rows, cols), jnp.int32), whole,
            pltpu.SemaphoreType.DMA((pieces, 4)),
            pltpu.SemaphoreType.DMA((pieces,)),
            pltpu.SemaphoreType.DMA((4,)),
        ]
        + [vmem(edge.shape) for edge in edges[3:]]
        + [
            level, level, level,
            compact, compact, compact, compact,
            row, row, row, row,
            vmem((rows, 4 * HEADS, LOW)),
            vmem((per, halves, 3, rows + 16, LANES)),
            vmem((rows, HEADS, 2 * LOW)),
        ]
        + [vmem((per, rows, cols))] * 12,
        compiler_params=pltpu.CompilerParams(vmem_limit_bytes=VMEM),
        name="step_and_bin",
    )(thick, depth, basins, *edges, *fields)


def close_kernel(scales, pieces, carries, *refs):
    count = pieces + carries
    sources, (over_ref, tend_ref), landed = (refs[:count], refs[count : count + 2], refs[count + 2 : 2 * count + 2])
    up_ref, run_ref, sem = refs[2 * count + 2 :]
    copies = [pltpu.make_async_copy(src, dst, sem.at[i]) for i, (src, dst) in enumerate(zip(sources, landed))]
    for copy in copies:
        copy.start()
    source = row_ids((2 * LOW, 2 * LOW))
    target = lane_ids((2 * LOW, 2 * LOW))
    after = ((source < LOW) & ((target >= LOW) | (source >= target))).astype(F32)
    for copy in copies:
        copy.wait()
    piece_refs, carry_refs = (landed[:pieces], landed[pieces:])
    share = piece_refs[0].shape[0]
    total = piece_refs[0][...]
    for ref in piece_refs[1:]:
        total = total + ref[...]
    total = total.reshape(share * HEADS, 2 * LOW)
    up_ref[...] = jnp.dot(total, after, precision=lax.Precision.HIGHEST, preferred_element_type=F32)
    run_ref[...] = total
    carry = jnp.zeros((HEADS, 2 * LOW), F32)
    for ref in carry_refs:
        carry = carry + ref[...]
    for b in range(B):
        above = jnp.zeros((share, LOW), F32)
        for high in reversed(range(HIGH)):
            head = b * HIGH + high
            rows = up_ref[pl.ds(head, share, HEADS), :]
            over_ref[b, :, high * LOW : (high + 1) * LOW] = (rows[:, :LOW] + above) * scales[0]
            above = above + rows[:, LOW:]
            rows = run_ref[pl.ds(head, share, HEADS), :] + carry[head : head + 1]
            tend_ref[b, :, high * LOW : (high + 1) * LOW] = rows[:, LOW:] * scales[1]


def close(pieces, carries, scales):
    share = pieces[0].shape[0]
    out = jax.ShapeDtypeStruct((B, share, C), F32)
    inputs = (*pieces, *carries)
    scratch = pltpu.VMEM((share * HEADS, 2 * LOW), F32)
    return pl.pallas_call(
        functools.partial(close_kernel, scales, len(pieces), len(carries)),
        in_specs=[pl.BlockSpec(memory_space=pl.ANY)] * len(inputs),
        out_shape=[out, out],
        scratch_shapes=[pltpu.VMEM(x.shape, F32) for x in inputs]
        + [scratch, scratch, pltpu.SemaphoreType.DMA((len(inputs),))],
        compiler_params=pltpu.CompilerParams(vmem_limit_bytes=VMEM),
        name="close_sums",
    )(*inputs)


def turn(count, step):
    return [(i, (i + step) % count) for i in range(count)]


def body(tracer, u_flow, v_flow, depth_levels, class_index, basin_index, level_thickness):
    levels, rows, cols = tracer.shape
    lons, lats = (lax.axis_size("lon"), lax.axis_size("lat"))
    up, down = pack_rows(tracer, v_flow, depth_levels)
    south = lax.ppermute(up, "lat", turn(lats, 1))
    ahead = lax.ppermute(down, "lat", turn(lats, -1))
    side = pack_columns(tracer, u_flow, depth_levels)
    west = lax.ppermute(side, "lon", turn(lons, 1))
    far = lax.ppermute(side, "lon", turn(lons, -1))
    tracer_next, block_total, *pieces = step_and_bin(
        lons,
        level_thickness,
        depth_levels,
        basin_index,
        (side, up, down, west, far, south, ahead),
        (tracer, u_flow, v_flow, class_index),
    )
    pieces = pieces[:1] + [lax.ppermute(pieces[d], "lon", turn(lons, d)) for d in range(1, lons)]
    lat = lax.axis_index("lat")
    carry = jnp.zeros((HEADS, 2 * LOW), F32)
    for d in range(1, lats):
        carry = carry + jnp.where(lat >= d, lax.ppermute(block_total, "lat", turn(lats, d)), 0.0)
    carries = [carry] + [lax.ppermute(carry, "lon", turn(lons, d)) for d in range(1, lons)]
    unit = 1.0 / math.sqrt(cols * lons * levels)
    overturning, tendency = close(pieces, carries, (16.0 * unit, 4.0 * unit))
    return (tracer_next, overturning, tendency)


def solution(mesh):
    return jax.shard_map(
        body,
        mesh=mesh,
        in_specs=(
            P("member", "lat", "lon"),
            P("member", "lat", "lon"),
            P("member", "lat", "lon"),
            P(("member", "lat"), "lon"),
            P("member", "lat", "lon"),
            P(("member", "lat"), "lon"),
            P(),
        ),
        out_specs=(
            P("member", "lat", "lon"),
            P("member", ("lat", "lon"), None),
            P("member", ("lat", "lon"), None),
        ),
        check_vma=False,
    )
```

```python
import functools
import math

import jax
import jax.numpy as jnp
from jax import lax
from jax.experimental import pallas as pl
from jax.experimental.pallas import tpu as pltpu
from jax.sharding import PartitionSpec as P

C = 192
B = 5
DIFFUSION = 0.1

LANES = 128
LOW = 64
HIGH = C // LOW
HEADS = 16
PER = 5
SLOTS = 5
VMEM = 64 << 20
F32 = jnp.float32
BF16 = jnp.bfloat16


def lane_ids(shape):
    return lax.broadcasted_iota(jnp.int32, shape, len(shape) - 1)


def row_ids(shape):
    return lax.broadcasted_iota(jnp.int32, shape, len(shape) - 2)


def flux_of(here, slope, bend, bend_ahead, speed):
    value = here + 0.5 * slope - jnp.where(speed > 0.0, bend, bend_ahead)
    return speed * value - DIFFUSION * slope


def sixth(behind, here, ahead):
    return ((ahead - here) - (here - behind)) * (1.0 / 6.0)


def rows_kernel(south_ref, north_ref, speed_ref, depth_ref, up_ref, down_ref):
    levels = south_ref.shape[0]
    rows = depth_ref.shape[0]

    def level(k, carry):
        here = pl.ds(k, 1)
        lower = jnp.where(k < depth_ref[0:8], south_ref[k], 0.0)
        upper = jnp.where(k < depth_ref[rows - 8 :], north_ref[k], 0.0)
        up_ref[0, here, :] = upper[6:7]
        up_ref[1, here, :] = upper[7:8]
        up_ref[2, here, :] = speed_ref[k, 7:8, :]
        down_ref[0, here, :] = lower[0:1]
        down_ref[1, here, :] = lower[1:2]
        return carry

    lax.fori_loop(0, levels, level, 0, unroll=15)
    up_ref[0, levels : levels + 1, :] = depth_ref[rows - 1 : rows].astype(F32)
    down_ref[0, levels : levels + 1, :] = depth_ref[0:1].astype(F32)


def pack_rows(tracer, v_flow, depth):
    levels, rows, cols = tracer.shape
    tall = (levels + 8) // 8 * 8
    shapes = [(3, tall, cols), (2, tall, cols)]
    return pl.pallas_call(
        rows_kernel,
        grid=(1,),
        in_specs=[
            pl.BlockSpec((levels, 8, cols), lambda i: (0, 0, 0)),
            pl.BlockSpec((levels, 8, cols), lambda i: (0, rows // 8 - 1, 0)),
            pl.BlockSpec((levels, 8, cols), lambda i: (0, rows // 8 - 1, 0)),
            pl.BlockSpec((rows, cols), lambda i: (0, 0)),
        ],
        out_specs=[pl.BlockSpec(s, lambda i: (0, 0, 0)) for s in shapes],
        out_shape=[jax.ShapeDtypeStruct(s, F32) for s in shapes],
        compiler_params=pltpu.CompilerParams(vmem_limit_bytes=VMEM),
        name="pack_rows",
    )(tracer, tracer, v_flow, depth)


def columns_kernel(tracer_ref, east_ref, depth_ref, side_ref):
    per, rows, cols = tracer_ref.shape
    step = pl.program_id(0)
    lanes = lane_ids((rows, LANES))
    owner, slot = (lanes // SLOTS, lanes % SLOTS)
    depth = depth_ref[...]
    near, away = (depth[:, :LANES], depth[:, cols - LANES :])
    deep = jnp.where(lanes < LANES // 2, near, away)
    value = pltpu.roll(deep.astype(F32), SLOTS * per + 2, 1)
    for q in range(per):
        k = step * per + q
        ends = jnp.where(lanes < LANES // 2, tracer_ref[q, :, :LANES], tracer_ref[q, :, cols - LANES :])
        turned = pltpu.roll(jnp.where(k < deep, ends, 0.0), SLOTS * q + 2, 1)
        turned = jnp.where(slot == SLOTS - 1, pltpu.roll(east_ref[q], SLOTS * q + SLOTS, 1), turned)
        value = jnp.where(owner == q, turned, value)
    side_ref[:, pl.ds(pl.multiple_of(step * LANES, LANES), LANES)] = value


def levels_of_tile(levels):
    return next(n for n in range((LANES - 3) // SLOTS, 0, -1) if levels % n == 0)


def pack_columns(tracer, u_flow, depth):
    levels, rows, cols = tracer.shape
    per = levels_of_tile(levels)
    tiles = levels // per
    return pl.pallas_call(
        columns_kernel,
        grid=(tiles,),
        in_specs=[
            pl.BlockSpec((per, rows, cols), lambda i: (i, 0, 0)),
            pl.BlockSpec((per, rows, LANES), lambda i: (i, 0, cols // LANES - 1)),
            pl.BlockSpec((rows, cols), lambda i: (0, 0)),
        ],
        out_specs=pl.BlockSpec((rows, tiles * LANES), lambda i: (0, 0)),
        out_shape=jax.ShapeDtypeStruct((rows, tiles * LANES), F32),
        compiler_params=pltpu.CompilerParams(vmem_limit_bytes=VMEM),
        name="pack_columns",
    )(tracer, u_flow, depth)


def main_kernel(
    thick_ref, depth_ref, basin_ref, side_ref, up_ref, down_ref,
    west_hbm, far_hbm, south_hbm, ahead_hbm, tracer_hbm, east_hbm, north_hbm, class_hbm,
    *refs,
):
    scratch = 26 + 12
    next_hbm, total_ref, *piece_refs = refs[: len(refs) - scratch]
    (
        tracer_ref, east_ref, north_ref, class_ref, next_ref, in_sem, out_sem, halo_sem,
        west_ref, far_ref, south_ref, ahead_ref,
        head_ref, zonal_ref, merid_ref, far_value, far_bend, west_slope, west_flux,
        ahead_value, ahead_bend, south_value, south_flux,
        sums_ref, tall_ref, share_ref,
    ) = refs[len(refs) - scratch : len(refs) - 12]
    stages = refs[len(refs) - 12 :]
    levels, rows, cols = tracer_ref.shape
    halves = cols // LANES
    per = stages[0].shape[0]
    chunks = levels // per
    parts = len(piece_refs)
    share = rows // parts
    place = lax.axis_index("lon")
    lat = lax.axis_index("lat")

    bounds = [(0, per)] + [(per * (2 * i + 1), min(2 * per, levels - per * (2 * i + 1))) for i in range(chunks // 2)]
    size = {n for _, n in bounds[1:]}
    assert len(size) == 1
    size = size.pop()

    def span(piece):
        if isinstance(piece, int) and piece == 0:
            return pl.ds(0, per)
        return pl.ds(per + (piece - 1) * size, size)

    sources = ((tracer_hbm, tracer_ref), (east_hbm, east_ref), (north_hbm, north_ref), (class_hbm, class_ref))
    halos = ((west_hbm, west_ref), (far_hbm, far_ref), (south_hbm, south_ref), (ahead_hbm, ahead_ref))

    def copies_in(piece):
        return [
            pltpu.make_async_copy(src.at[span(piece)], dst.at[span(piece)], in_sem.at[piece, i])
            for i, (src, dst) in enumerate(sources)
        ]

    def copy_out(piece):
        return pltpu.make_async_copy(next_ref.at[span(piece)], next_hbm.at[span(piece)], out_sem.at[piece])

    pieces = len(bounds)
    edges = [pltpu.make_async_copy(src, dst, halo_sem.at[i]) for i, (src, dst) in enumerate(halos)]
    for copy in edges:
        copy.start()
    for piece in range(2):
        for copy in copies_in(piece):
            copy.start()
    for copy in edges:
        copy.wait()

    span_of = levels_of_tile(levels)
    tiles = levels // span_of
    lanes = lane_ids((rows, LANES))
    slots = lanes % SLOTS
    depth = depth_ref[...].astype(F32)
    has_west, has_far = (place > 0, place < parts - 1)
    for tile in range(tiles):
        part = slice(tile * LANES, (tile + 1) * LANES)
        own = side_ref[:, part]
        west = jnp.where(has_west, west_ref[:, part], 0.0)
        far = jnp.where(has_far, far_ref[:, part], 0.0)
        speed = pltpu.roll(west, LANES - SLOTS + 2, 1)

        def beside(x):
            return pltpu.roll(x, LANES - 1, 1)

        def curve(x):
            return sixth(pltpu.roll(x, 1, 1), x, beside(x))

        right = jnp.where(slots < 2, own, far)
        far_value[:, part] = right
        far_bend[:, part] = curve(right)
        left = jnp.where(slots < 2, west, own)
        slope = beside(left) - left
        west_slope[:, part] = slope
        bend = curve(left)
        flux = flux_of(left, slope, bend, beside(bend), speed)
        lane = SLOTS * span_of
        faces = jnp.minimum(west[:, lane + 1 : lane + 2], depth[:, :1])
        west_flux[:, part] = jnp.where((lanes // SLOTS + tile * span_of).astype(F32) < faces, flux, 0.0)
        if tile == 0:
            wide = lane_ids((rows, cols))
            after = jnp.where(wide == cols - 1, far[:, lane + 2 : lane + 3], pltpu.roll(depth, cols - 1, 1))
            zonal_ref[...] = jnp.minimum(depth, after).astype(jnp.int32)

    has_south, has_ahead = (lat > 0, lat < lax.axis_size("lat") - 1)
    first, second = (down_ref[0], down_ref[1])
    here = jnp.where(has_south, south_ref[1], 0.0)
    behind = jnp.where(has_south, south_ref[0], 0.0)
    speed = jnp.where(has_south, south_ref[2], 0.0)
    beyond = jnp.where(has_ahead, ahead_ref[0], 0.0)
    south_value[...] = here
    ahead_value[...] = beyond
    ahead_bend[...] = sixth(up_ref[1], beyond, jnp.where(has_ahead, ahead_ref[1], 0.0))
    flux = flux_of(here, first - here, sixth(behind, here, first), sixth(here, first, second), speed)
    faces = jnp.minimum(behind[levels : levels + 1, :], depth[0:1])
    south_flux[...] = jnp.where(row_ids(flux.shape).astype(F32) < faces, flux, 0.0)
    above = pltpu.roll(depth, rows - 1, 0)
    above = jnp.where(row_ids((rows, cols)) == rows - 1, beyond[levels : levels + 1, :], above)
    merid_ref[...] = jnp.minimum(depth, above).astype(jnp.int32)
    head_ref[...] = basin_ref[...] * HIGH

    top = 8
    inner = pl.ds(top, rows)

    def level(chunk, q, stage):
        flow_hi, flow_lo, gain_hi, gain_lo, head_key, low_key = stage
        k = chunk * per + q
        thick = thick_ref[k]
        here = pl.ds(k, 1)
        edge = lane_ids((rows, LANES))
        at_end, at_start = (edge == LANES - 1, edge == 0)

        def split(array):
            return [array[:, h * LANES : (h + 1) * LANES] for h in range(halves)]

        def turn_back(blocks, outside):
            turned = [pltpu.roll(x, LANES - 1, 1) for x in blocks] + [outside]
            return [jnp.where(at_end, turned[h + 1], turned[h]) for h in range(halves)]

        def turn_on(blocks, outside):
            turned = [outside] + [pltpu.roll(x, 1, 1) for x in blocks]
            return [jnp.where(at_start, turned[h], turned[h + 1]) for h in range(halves)]

        tile = pl.ds(pl.multiple_of(k // span_of * LANES, LANES), LANES)
        slot = SLOTS * (k % span_of)

        def to_end(ref):
            return pltpu.roll(ref[:, tile], LANES - 3 - slot, 1)

        def to_start(ref):
            return pltpu.roll(ref[:, tile], LANES - 1 - slot, 1)

        depth = split(depth_ref[...])
        raw = split(tracer_ref[k])
        wet = [k < d for d in depth]
        masked = [jnp.where(w, x, 0.0) for w, x in zip(wet, raw)]

        ahead = turn_back(masked, to_end(far_value))
        slope = [a - x for a, x in zip(ahead, masked)]
        slope_behind = turn_on(slope, to_start(west_slope))
        bend = [(a - b) * (1.0 / 6.0) for a, b in zip(slope, slope_behind)]
        bend_ahead = turn_back(bend, to_end(far_bend))
        speed = split(east_ref[k])
        shut = [k >= d for d in split(zonal_ref[...])]
        flux = [
            jnp.where(s, 0.0, flux_of(*x)) for s, *x in zip(shut, masked, slope, bend, bend_ahead, speed)
        ]
        flux_behind = turn_on(flux, to_start(west_flux))
        left_over = [m - (a - b) for m, a, b in zip(masked, flux, flux_behind)]

        north = split(north_ref[k])
        shut = [k >= d for d in split(merid_ref[...])]
        classes = split(class_ref[k])
        heads = split(head_ref[...])
        below, over = (split(south_value[here, :]), split(ahead_value[here, :]))
        over_bend, below_flux = (split(ahead_bend[here, :]), split(south_flux[here, :]))
        for h in range(halves):
            part = slice(h * LANES, (h + 1) * LANES)
            rows_of = tall_ref.at[q, h]
            rows_of[0, inner, :] = masked[h]
            rows_of[0, top - 1 : top, :] = below[h]
            rows_of[0, top + rows : top + rows + 1, :] = over[h]
            slope = rows_of[0, pl.ds(top + 1, rows), :] - masked[h]
            slope_behind = masked[h] - rows_of[0, pl.ds(top - 1, rows), :]
            bend = (slope - slope_behind) * (1.0 / 6.0)
            rows_of[1, inner, :] = bend
            rows_of[1, top + rows : top + rows + 1, :] = over_bend[h]
            bend_ahead = rows_of[1, pl.ds(top + 1, rows), :]
            flux = jnp.where(shut[h], 0.0, flux_of(masked[h], slope, bend, bend_ahead, north[h]))
            rows_of[2, inner, :] = flux
            rows_of[2, top - 1 : top, :] = below_flux[h]
            flux_behind = rows_of[2, pl.ds(top - 1, rows), :]
            updated = jnp.where(wet[h], left_over[h] - (flux - flux_behind), 0.0)
            next_ref[k, :, part] = updated
            flow = jnp.where(shut[h], 0.0, north[h] * thick)
            gain = (updated - masked[h]) * thick
            upper = flow.astype(BF16).astype(F32)
            flow_hi[q, :, part] = flow
            flow_lo[q, :, part] = flow - upper
            upper = gain.astype(BF16).astype(F32)
            gain_hi[q, :, part] = gain
            gain_lo[q, :, part] = gain - upper
            head_key[q, :, part] = (heads[h] + (classes[h] >> 6)).astype(F32)
            low_key[q, :, part] = (classes[h] & (LOW - 1)).astype(F32)

    half = HEADS // 2
    order = row_ids((HEADS, cols))
    heads = [(order % half + g * half).astype(F32).astype(BF16) for g in range(2)]
    lows = row_ids((LOW, cols)).astype(F32).astype(BF16)
    ones = jnp.ones((LOW, cols), BF16)
    none = jnp.zeros((LOW, cols), BF16)

    def spread(ref, q, r, count):
        return jnp.broadcast_to(ref[q, r : r + 1, :], (count, cols))

    def bin_row(r, stage, fresh):
        *terms, head_key, low_key = stage
        first, second = ([], [])
        for q in range(per):
            key = spread(head_key, q, r, HEADS).astype(BF16)
            hot = [key == g for g in heads]
            tiles = []
            for upper, lower in (terms[:2], terms[2:]):
                value = jnp.concatenate([spread(upper, q, r, half), spread(lower, q, r, half)], 0).astype(BF16)
                tiles += [jnp.where(g, value, none[:HEADS]) for g in hot]
            first.append(jnp.concatenate(tiles, 0))
            second.append(jnp.where(spread(low_key, q, r, LOW).astype(BF16) == lows, ones, none))
        total = lax.dot_general(
            jnp.concatenate(first, 1),
            jnp.concatenate(second, 1),
            (((1,), (1,)), ((), ())),
            preferred_element_type=F32,
        )
        sums_ref[r] = jnp.where(fresh, total, total + sums_ref[r])

    both = (stages[:6], stages[6:])

    def work(chunk, stage_in, stage_out, fresh=None):
        done = 0
        for q in range(per):
            until = (q + 1) * rows // per
            if stage_out is not None:
                for r in range(done, until):
                    bin_row(r, stage_out, fresh)
            if stage_in is not None:
                level(chunk, q, stage_in)
            done = until

    for copy in copies_in(0):
        copy.wait()
    work(0, both[0], None)
    copy_out(0).start()

    def pair(i, carry):
        @pl.when(i < pieces - 2)
        def _():
            for copy in copies_in(i + 2):
                copy.start()

        for copy in copies_in(i + 1):
            copy.wait()
        for j in range(size // per):
            work(2 * i + 1 + j, both[(1 + j) % 2], both[j % 2], 2 * i + j == 0)
        copy_out(i + 1).start()
        return carry

    lax.fori_loop(0, pieces - 1, pair, 0)
    work(0, None, both[(chunks - 1) % 2], place < 0)
    running = jnp.zeros((HEADS, LOW), F32)
    for r in range(rows):
        tiles = [sums_ref[r, pl.ds(i * half, half)] for i in range(8)]
        joined = [tiles[2 * i] + tiles[2 * i + 1] for i in range(4)]
        flow = jnp.concatenate(joined[:2], 0)
        running = running + jnp.concatenate(joined[2:], 0)
        share_ref[r] = jnp.concatenate([flow, running], 1)
    for d in range(parts):
        owner = lax.rem(place + d, parts)
        piece_refs[d][...] = share_ref[pl.ds(owner * share, share)]
    total_ref[...] = share_ref[rows - 1]
    for piece in range(pieces):
        copy_out(piece).wait()


def step_and_bin(parts, thick, depth, basins, edges, fields):
    levels, rows, cols = fields[0].shape
    per = next(n for n in range(PER, 0, -1) if levels % n == 0)
    pieces = 1 + levels // per // 2
    halves = cols // LANES
    tall = edges[1].shape[1]
    share = rows // parts

    def vmem(shape, dtype=F32):
        return pltpu.VMEM(shape, dtype)

    whole = vmem((levels, rows, cols))
    compact = vmem((rows, levels // levels_of_tile(levels) * LANES))
    row = vmem((tall, cols))
    level = vmem((rows, cols), jnp.int32)
    piece = (share, HEADS, 2 * LOW)
    return pl.pallas_call(
        main_kernel,
        in_specs=[pl.BlockSpec(memory_space=pltpu.SMEM)]
        + [pl.BlockSpec(memory_space=pltpu.VMEM)] * 5
        + [pl.BlockSpec(memory_space=pl.ANY)] * 8,
        out_specs=[pl.BlockSpec(memory_space=pl.ANY)] + [pl.BlockSpec(memory_space=pltpu.VMEM)] * (parts + 1),
        out_shape=[jax.ShapeDtypeStruct(s, F32) for s in [(levels, rows, cols), piece[1:]] + [piece] * parts],
        scratch_shapes=[
            whole, whole, whole, vmem((levels, rows, cols), jnp.int32), whole,
            pltpu.SemaphoreType.DMA((pieces, 4)),
            pltpu.SemaphoreType.DMA((pieces,)),
            pltpu.SemaphoreType.DMA((4,)),
        ]
        + [vmem(edge.shape) for edge in edges[3:]]
        + [
            level, level, level,
            compact, compact, compact, compact,
            row, row, row, row,
            vmem((rows, 4 * HEADS, LOW)),
            vmem((per, halves, 3, rows + 16, LANES)),
            vmem((rows, HEADS, 2 * LOW)),
        ]
        + [vmem((per, rows, cols))] * 12,
        compiler_params=pltpu.CompilerParams(vmem_limit_bytes=VMEM),
        name="step_and_bin",
    )(thick, depth, basins, *edges, *fields)


def close_kernel(scales, pieces, carries, *refs):
    count = pieces + carries
    sources, (over_ref, tend_ref), landed = (refs[:count], refs[count : count + 2], refs[count + 2 : 2 * count + 2])
    up_ref, run_ref, sem = refs[2 * count + 2 :]
    copies = [pltpu.make_async_copy(src, dst, sem.at[i]) for i, (src, dst) in enumerate(zip(sources, landed))]
    for copy in copies:
        copy.start()
    source = row_ids((2 * LOW, 2 * LOW))
    target = lane_ids((2 * LOW, 2 * LOW))
    after = ((source < LOW) & ((target >= LOW) | (source >= target))).astype(F32)
    for copy in copies:
        copy.wait()
    piece_refs, carry_refs = (landed[:pieces], landed[pieces:])
    share = piece_refs[0].shape[0]
    total = piece_refs[0][...]
    for ref in piece_refs[1:]:
        total = total + ref[...]
    total = total.reshape(share * HEADS, 2 * LOW)
    up_ref[...] = jnp.dot(total, after, precision=lax.Precision.HIGHEST, preferred_element_type=F32)
    run_ref[...] = total
    carry = jnp.zeros((HEADS, 2 * LOW), F32)
    for ref in carry_refs:
        carry = carry + ref[...]
    for b in range(B):
        above = jnp.zeros((share, LOW), F32)
        for high in reversed(range(HIGH)):
            head = b * HIGH + high
            rows = up_ref[pl.ds(head, share, HEADS), :]
            over_ref[b, :, high * LOW : (high + 1) * LOW] = (rows[:, :LOW] + above) * scales[0]
            above = above + rows[:, LOW:]
            rows = run_ref[pl.ds(head, share, HEADS), :] + carry[head : head + 1]
            tend_ref[b, :, high * LOW : (high + 1) * LOW] = rows[:, LOW:] * scales[1]


def close(pieces, carries, scales):
    share = pieces[0].shape[0]
    out = jax.ShapeDtypeStruct((B, share, C), F32)
    inputs = (*pieces, *carries)
    scratch = pltpu.VMEM((share * HEADS, 2 * LOW), F32)
    return pl.pallas_call(
        functools.partial(close_kernel, scales, len(pieces), len(carries)),
        in_specs=[pl.BlockSpec(memory_space=pl.ANY)] * len(inputs),
        out_shape=[out, out],
        scratch_shapes=[pltpu.VMEM(x.shape, F32) for x in inputs]
        + [scratch, scratch, pltpu.SemaphoreType.DMA((len(inputs),))],
        compiler_params=pltpu.CompilerParams(vmem_limit_bytes=VMEM),
        name="close_sums",
    )(*inputs)


def turn(count, step):
    return [(i, (i + step) % count) for i in range(count)]


def body(tracer, u_flow, v_flow, depth_levels, class_index, basin_index, level_thickness):
    levels, rows, cols = tracer.shape
    lons, lats = (lax.axis_size("lon"), lax.axis_size("lat"))
    up, down = pack_rows(tracer, v_flow, depth_levels)
    south = lax.ppermute(up, "lat", turn(lats, 1))
    ahead = lax.ppermute(down, "lat", turn(lats, -1))
    side = pack_columns(tracer, u_flow, depth_levels)
    west = lax.ppermute(side, "lon", turn(lons, 1))
    far = lax.ppermute(side, "lon", turn(lons, -1))
    tracer_next, block_total, *pieces = step_and_bin(
        lons,
        level_thickness,
        depth_levels,
        basin_index,
        (side, up, down, west, far, south, ahead),
        (tracer, u_flow, v_flow, class_index),
    )
    pieces = pieces[:1] + [lax.ppermute(pieces[d], "lon", turn(lons, d)) for d in range(1, lons)]
    lat = lax.axis_index("lat")
    carry = jnp.zeros((HEADS, 2 * LOW), F32)
    for d in range(1, lats):
        carry = carry + jnp.where(lat >= d, lax.ppermute(block_total, "lat", turn(lats, d)), 0.0)
    carries = [carry]
    if lons & (lons - 1) == 0:
        bit = 1
        while bit < lons:
            carry = sum(carries)
            carries = [carry, lax.ppermute(carry, "lon", [(i, i ^ bit) for i in range(lons)])]
            bit *= 2
    else:
        carries += [lax.ppermute(carry, "lon", turn(lons, d)) for d in range(1, lons)]
    unit = 1.0 / math.sqrt(cols * lons * levels)
    overturning, tendency = close(pieces, carries, (16.0 * unit, 4.0 * unit))
    return (tracer_next, overturning, tendency)


def solution(mesh):
    return jax.shard_map(
        body,
        mesh=mesh,
        in_specs=(
            P("member", "lat", "lon"),
            P("member", "lat", "lon"),
            P("member", "lat", "lon"),
            P(("member", "lat"), "lon"),
            P("member", "lat", "lon"),
            P(("member", "lat"), "lon"),
            P(),
        ),
        out_specs=(
            P("member", "lat", "lon"),
            P("member", ("lat", "lon"), None),
            P("member", ("lat", "lon"), None),
        ),
        check_vma=False,
    )
```
